256 devices in a mesh: px: 16 (over y, x), py: 16 (over z, core).
Axes of the slice: x: 4, y: 4, z: 8, core: 2. Of those that a mesh axis runs over, the one named last changes fastest.
Arguments:
- body_force: float32 [16, 16, 3, 4096], P('px', 'py'), may hold values from -6 to 6
- fault_slip: float32 [16, 16, 3, 512], P('px', 'py'), may hold values from -6 to 6
- elem_nodes: int32 [16, 16, 27, 512], P('px', 'py'), may hold values from 0 to 5119
- moduli: float32 [16, 16, 2, 512], P('px', 'py'), may hold values from 0.5 to 5
- stiff_ref: float32 [2, 81, 81], replicated
- block_inv: float32 [16, 16, 9, 4096], P('px', 'py')
- send_nodes: int32 [16, 16, 4, 256], P('px', 'py'), may hold values from 0 to 4095
- fault_nodes: int32 [16, 16, 2, 512], P('px', 'py'), may hold values from 0 to 4095
Outputs:
- displacement: float32 [16, 16, 3, 4096], P('px', 'py')
- multiplier: float32 [16, 16, 3, 512], P('px', 'py')
The draws below stay inside these ranges and needn't reach their ends.
Inputs may be any that keep to these rules, and one draw needn't show every extreme that they name: `elem_nodes`: slots below 4096 are owned nodes; slot 4096 + k * 256 + i is entry i of ghost block k (k = 0 .. 3 from px-1, px+1, py-1, py+1). `send_nodes`: owned node numbers; entries may repeat. `fault_nodes`: owned node numbers; entries may repeat.
All inputs are finite; a program needn't handle non-finite values.
Results may differ from the reference program's by a relative error of at most 0.00018.
Values sent between devices are 32-bit elements; how exact they have to be, the bound alone decides.
No kernel may reach another device: no remote copies, remote signals or barrier semaphores. Data moves between devices by JAX's collectives and lax.ppermute only.
A program may use at most 64 MiB of HBM per device.

```python
import math
import jax
import jax.numpy as jnp
from jax import lax

NEL = 512
NN = 4096
NB = 256
NF = 512
ITERS = 3
N_PX = 16
N_PY = 16


def draw_stiff_ref(key, part):
    key = jax.random.fold_in(key, 11)
    first, second = jax.random.split(key)
    off = 0.03 * jax.random.normal(first, (2, 81, 81), jnp.float32)
    symmetric = off + jnp.swapaxes(off, 1, 2)
    diagonal = jax.random.uniform(second, (2, 81), jnp.float32, 4.0, 6.0)
    identity = jnp.eye(81, dtype=jnp.float32)
    return symmetric * (1.0 - identity) + diagonal[:, :, None] * identity


def draw_block_inv(key, part):
    key = jax.random.fold_in(key, 23)
    first, second = jax.random.split(key)
    logs = jax.random.uniform(first, (N_PX, N_PY, 1, 1, NN), jnp.float32, jnp.log(0.03), jnp.log(0.3))
    scales = jnp.exp(logs)
    mixing = 0.2 * jax.random.normal(second, (N_PX, N_PY, 3, 3, NN), jnp.float32)
    identity = jnp.eye(3, dtype=jnp.float32)[:, :, None]
    blocks = scales * (identity + (1.0 - identity) * mixing)
    return blocks.reshape(N_PX, N_PY, 9, NN)


def set_ends(drawn, rng, low, largest):
    longest = drawn.shape.index(max(drawn.shape))
    spots = []
    for shift in (0, 1):
        where = [jax.random.randint(jax.random.fold_in(rng, axis), (), 0, length) for axis, length in enumerate(drawn.shape)]
        where[longest] = (where[longest] + shift) % drawn.shape[longest]
        spots.append(tuple(where))
    return drawn.at[spots[0]].set(low).at[spots[1]].set(largest)


def shard_levels(key, dims, cuts, smallest, top_value):
    loudness = 1.0
    for dim, shards_of in cuts:
        draws = jax.random.uniform(jax.random.fold_in(jax.random.fold_in(key, 6), dim), (shards_of,), jnp.float32, smallest / len(cuts), top_value / len(cuts))
        loudness = loudness * jnp.repeat(jnp.exp(draws), dims[dim] // shards_of).reshape((-1,) + (1,) * (len(dims) - 1 - dim))
    return loudness


def gaussian(own_key, shape, scale, most, cuts=(), held_as=jnp.bfloat16):
    drawn = jax.random.normal(own_key, shape, jnp.float32) * scale
    if len(cuts) > 0:
        drawn = shard_levels(own_key, shape, cuts, -0.22, 0.18) * drawn
    return jnp.clip(drawn, min=-most, max=most).astype(held_as)


def setup_inputs(seed: int = 0) -> dict:
    arg_keys = jax.random.split(jax.random.key(seed), 9)
    return {
        "body_force": gaussian(arg_keys[0], (N_PX, N_PY, 3, NN), 1.0, 6.0, ((0, 16), (1, 16)), jnp.float32),
        "fault_slip": gaussian(arg_keys[1], (N_PX, N_PY, 3, NF), 1.0, 6.0, ((0, 16), (1, 16)), jnp.float32),
        "elem_nodes": set_ends(jax.random.randint(arg_keys[2], (N_PX, N_PY, 27, NEL), 0, NN + 4 * NB), jax.random.fold_in(arg_keys[2], 1), 0, (NN + 4 * NB) - 1).astype(jnp.int32),
        "moduli": jnp.clip(jnp.exp(math.log(5.0) - 2.3025851 * jax.random.uniform(arg_keys[3], (N_PX, N_PY, 2, NEL), jnp.float32) ** shard_levels(arg_keys[3], (N_PX, N_PY, 2, NEL), ((0, 16), (1, 16)), -0.2, 0.2)), 0.5, 5.0),
        "stiff_ref": draw_stiff_ref(jax.random.fold_in(arg_keys[8], 71), 0),
        "block_inv": draw_block_inv(jax.random.fold_in(arg_keys[8], 71), 0),
        "send_nodes": set_ends(jax.random.randint(arg_keys[6], (N_PX, N_PY, 4, NB), 0, NN), jax.random.fold_in(arg_keys[6], 1), 0, NN - 1).astype(jnp.int32),
        "fault_nodes": set_ends(jax.random.randint(arg_keys[7], (N_PX, N_PY, 2, NF), 0, NN), jax.random.fold_in(arg_keys[7], 1), 0, NN - 1).astype(jnp.int32),
    }


highest = lax.Precision.HIGHEST

def precondition(block_inv, field):
    blocks = block_inv.reshape(block_inv.shape[:-2] + (3, 3, block_inv.shape[-1]))
    return lax.optimization_barrier(jnp.sum(blocks * field[..., None, :, :], axis=-2))

def from_lower(array, axis):
    zeros = jnp.zeros_like(lax.slice_in_dim(array, 0, 1, axis=axis))
    return jnp.concatenate([zeros, lax.slice_in_dim(array, 0, array.shape[axis] - 1, axis=axis)], axis)

def from_upper(array, axis):
    zeros = jnp.zeros_like(lax.slice_in_dim(array, 0, 1, axis=axis))
    return jnp.concatenate([lax.slice_in_dim(array, 1, array.shape[axis], axis=axis), zeros], axis)

def partner(array):
    shape = array.shape
    paired = array.reshape((shape[0] // 2, 2) + shape[1:])
    return paired[:, ::-1].reshape(shape)

def devices(func):
    return jax.vmap(jax.vmap(func))

def pick(field, index):
    return field[:, index]

def add_at(field, index, value):
    return field.at[:, index].add(value)

def element_apply(extended, nodes, moduli, stiff_ref):
    count = nodes.shape[1]
    local = extended[:, nodes].reshape(81, count)
    first = jnp.dot(stiff_ref[0], local, precision=highest)
    second = jnp.dot(stiff_ref[1], local, precision=highest)
    result = moduli[0] * first + moduli[1] * second
    return jnp.zeros(extended.shape, jnp.float32).at[:, nodes].add(result.reshape(3, 27, count))

def operator(disp, mult, elem_nodes, moduli, stiff_ref, send_nodes, fault_nodes):
    owned_count = disp.shape[-1]
    width = send_nodes.shape[-1]
    boundary = devices(pick)(disp, send_nodes)
    ghosts = [from_lower(boundary[..., 1, :], 0), from_upper(boundary[..., 0, :], 0), from_lower(boundary[..., 3, :], 1), from_upper(boundary[..., 2, :], 1)]
    extended = jnp.concatenate([disp] + ghosts, axis=-1)
    shape = extended.shape
    flat = lax.map(lambda item: element_apply(item[0], item[1], item[2], stiff_ref), (extended.reshape((-1,) + shape[2:]), elem_nodes.reshape((-1,) + elem_nodes.shape[2:]), moduli.reshape((-1,) + moduli.shape[2:])))
    applied = flat.reshape(shape)
    owned = applied[..., :owned_count]
    blocks = [applied[..., owned_count + side * width:owned_count + (side + 1) * width] for side in range(4)]
    returned = [from_lower(blocks[1], 0), from_upper(blocks[0], 0), from_lower(blocks[3], 1), from_upper(blocks[2], 1)]
    for side in range(4):
        owned = devices(add_at)(owned, send_nodes[:, :, side], returned[side])
    own_ids = fault_nodes[:, :, 0]
    peer_ids = fault_nodes[:, :, 1]
    peer_disp = devices(pick)(disp, peer_ids)
    owned = devices(add_at)(owned, own_ids, mult)
    owned = devices(add_at)(owned, peer_ids, -partner(mult))
    jump = devices(pick)(disp, own_ids) - partner(peer_disp)
    return (owned, jump)

def inner(first, second):
    return jnp.sum(first[0] * second[0]) + jnp.sum(first[1] * second[1])

def least_squares(columns, beta):
    cosines, sines, upper = ([], [], [])
    target = [beta] + [jnp.zeros_like(beta) for later in columns]
    for position, column in enumerate(columns):
        column = list(column)
        for earlier in range(position):
            top = cosines[earlier] * column[earlier] + sines[earlier] * column[earlier + 1]
            below = -sines[earlier] * column[earlier] + cosines[earlier] * column[earlier + 1]
            column[earlier] = top
            column[earlier + 1] = below
        pivot = column[position]
        under = column[position + 1]
        radius = jnp.sqrt(pivot * pivot + under * under)
        cosine = pivot / radius
        sine = under / radius
        column[position] = radius
        cosines.append(cosine)
        sines.append(sine)
        target[position + 1] = -sine * target[position]
        target[position] = cosine * target[position]
        upper.append(column)
    count = len(columns)
    coeffs = [None] * count
    for row_index in reversed(range(count)):
        total = target[row_index]
        for later in range(row_index + 1, count):
            total = total - upper[later][row_index] * coeffs[later]
        coeffs[row_index] = total / upper[row_index][row_index]
    return coeffs

def reference(body_force, fault_slip, elem_nodes, moduli, stiff_ref, block_inv, send_nodes, fault_nodes):
    rhs = (body_force, fault_slip)
    beta = jnp.sqrt(inner(rhs, rhs))
    basis = [(body_force / beta, fault_slip / beta)]
    columns = []
    for position in range(ITERS):
        current = basis[-1]
        image = operator(precondition(block_inv, current[0]), current[1], elem_nodes, moduli, stiff_ref, send_nodes, fault_nodes)
        column = []
        for vector in basis:
            entry = inner(image, vector)
            image = (image[0] - entry * vector[0], image[1] - entry * vector[1])
            column.append(entry)
        norm = jnp.sqrt(inner(image, image))
        column.append(norm)
        columns.append(column)
        basis.append((image[0] / norm, image[1] / norm))
    coeffs = least_squares(columns, beta)
    combo_disp = sum((coeffs[index_pos] * basis[index_pos][0] for index_pos in range(ITERS)))
    combo_mult = sum((coeffs[index_pos] * basis[index_pos][1] for index_pos in range(ITERS)))
    return (precondition(block_inv, combo_disp), combo_mult)
```

```python
import jax
import jax.numpy as jnp
from jax import lax
from jax.experimental import pallas as pl
from jax.experimental.pallas import tpu as pltpu
from jax.sharding import PartitionSpec as P

ITERS = 3
LANES = 128
ROWS = 32
PIVOT_MIN = 0.01
f32, bf16, i32 = jnp.float32, jnp.bfloat16, jnp.int32
highest = lax.Precision.HIGHEST

VMEM = pl.BlockSpec(memory_space=pltpu.VMEM)
SMEM = pl.BlockSpec(memory_space=pltpu.SMEM)


def shape(*dims):
    return jax.ShapeDtypeStruct(dims, f32)


def call(kernel, outs, args, scratch=(), smem_first=False, flops=2_000_000):
    specs = [VMEM] * len(args)
    if smem_first:
        specs[0] = SMEM
    return pl.pallas_call(
        kernel,
        out_shape=outs,
        in_specs=specs,
        out_specs=[VMEM] * len(outs),
        scratch_shapes=list(scratch),
        compiler_params=pltpu.CompilerParams(vmem_limit_bytes=32 * 1024 * 1024),
        cost_estimate=pl.CostEstimate(flops=flops, bytes_accessed=1_000_000, transcendentals=0),
    )(*args)


def take_lanes(row, lanes):
    return jnp.take_along_axis(
        jnp.broadcast_to(row, lanes.shape), lanes, axis=1, mode="promise_in_bounds"
    )


def gather_rows(table, first, count, high, low, start):
    acc = [list(per) for per in start]
    for r in range(count):
        rows = [table(c, r) for c in range(3)]
        for n in range(len(high)):
            here = high[n] == r + first
            for c in range(3):
                acc[n][c] = jnp.where(here, take_lanes(rows[c], low[n]), acc[n][c])
    return acc


def one_hot_low(low_row):
    width = low_row.shape[1]
    rows = lax.broadcasted_iota(i32, (256, width), 0)
    return jnp.where(rows == low_row, 1.0, 0.0).astype(bf16)


def spread_owned(high_row, values):
    width = high_row.shape[1]
    rows = lax.broadcasted_iota(i32, (16, width), 0)
    here = rows == high_row
    upper, lower = [], []
    for value in values:
        top = value.astype(bf16).astype(f32)
        upper.append(jnp.where(here, top, 0.0))
        lower.append(jnp.where(here, value - top, 0.0))
    return jnp.concatenate(upper + lower, axis=0).astype(bf16)


def spread_ghost(high_row, values):
    width = high_row.shape[1]
    rows = lax.broadcasted_iota(i32, (16, width), 0)
    here = (rows < 12) & ((rows & 3) + 16 == high_row)
    tops = [value.astype(bf16).astype(f32) for value in values]
    rests = [value - top for value, top in zip(values, tops)]
    parts = []
    for v in (tops, rests):
        whole = jnp.where(rows < 4, v[0], jnp.where(rows < 8, v[1], v[2]))
        parts.append(jnp.where(here, whole, 0.0))
    return jnp.concatenate(parts, axis=0).astype(bf16)


def times_one_hot(spread, one_hot):
    return lax.dot_general(
        spread, one_hot, (((1,), (1,)), ((), ())), preferred_element_type=f32
    )


def send_payloads(par, u_ref, m_rows, sf, pay_e, pay_o, pay_f, pay_b, uown):
    high = [sf[8 * n : 8 * n + 8, :] >> 7 for n in range(2)]
    low = [sf[8 * n : 8 * n + 8, :] & 127 for n in range(2)]
    zero = jnp.zeros((8, LANES), f32)
    got = gather_rows(
        lambda c, r: u_ref[c, r : r + 1, :], 0, ROWS, high, low, [[zero] * 3, [zero] * 3]
    )
    pad = jnp.zeros((2, LANES), f32)
    sides = [
        jnp.concatenate([got[0][c][2 * s : 2 * s + 2, :] for c in range(3)] + [pad], axis=0)
        for s in range(4)
    ]
    odd = par == 1
    pay_e[0:8, :] = jnp.where(odd, sides[0], sides[1])
    pay_o[...] = jnp.where(odd, sides[1], sides[0])
    pay_b[...] = sides[2]
    pay_f[...] = sides[3]
    for c in range(3):
        pay_e[8 + 4 * c : 12 + 4 * c, :] = got[1][c][0:4, :]
        uown[4 * c : 4 * c + 4, :] = got[1][c][4:8, :]
    pay_e[20:32, :] = m_rows


def apply_blocks(inv_ref, w_ref, u_ref):
    w = [w_ref[c] for c in range(3)]
    for i in range(3):
        u_ref[i] = inv_ref[3 * i] * w[0] + inv_ref[3 * i + 1] * w[1] + inv_ref[3 * i + 2] * w[2]


def from_sides(flags, e, o, f, b):
    odd = flags[0] == 1
    zero = jnp.zeros((8, LANES), f32)
    e, o = e[0:8, :], o[...]
    return [
        jnp.where(flags[1] == 1, jnp.where(odd, e, o), zero),
        jnp.where(flags[2] == 1, jnp.where(odd, o, e), zero),
        jnp.where(flags[3] == 1, f[...], zero),
        jnp.where(flags[4] == 1, b[...], zero),
    ]


def first_kernel(flags, load, slip, inv, send, fault, w, m, inv_out, u, sf, pay_e, pay_o, pay_f, pay_b, uown):
    for r in range(ROWS):
        lanes = slice(LANES * r, LANES * r + LANES)
        for c in range(3):
            w[c, r : r + 1, :] = load[c : c + 1, lanes]
        for k in range(9):
            inv_out[k, r : r + 1, :] = inv[k : k + 1, lanes]
    for c in range(3):
        for t in range(4):
            m[4 * c + t : 4 * c + t + 1, :] = slip[c : c + 1, LANES * t : LANES * t + LANES]
    for s in range(4):
        for h in range(2):
            sf[2 * s + h : 2 * s + h + 1, :] = send[s : s + 1, LANES * h : LANES * h + LANES]
    for t in range(4):
        lanes = slice(LANES * t, LANES * t + LANES)
        sf[8 + t : 9 + t, :] = fault[1:2, lanes]
        sf[12 + t : 13 + t, :] = fault[0:1, lanes]
    apply_blocks(inv_out, w, u)
    send_payloads(flags[0], u, m[...], sf, pay_e, pay_o, pay_f, pay_b, uown)


def prepare_kernel(nodes, stiff, nodes_out, stiff_out):
    nodes_out[27:32, :] = jnp.zeros((5, 512), i32)
    nodes_out[0:27, :] = nodes[...]
    rows = lax.broadcasted_iota(i32, (96, 81), 0)
    cols = lax.broadcasted_iota(i32, (96, 81), 1)
    a = rows & 31
    widen = jnp.where(((rows >> 5) * 27 + a == cols) & (a < 27), 1.0, 0.0)
    for k in range(2):
        part = jnp.dot(widen, stiff[k], precision=highest, preferred_element_type=f32)
        stiff_out[:, 96 * k : 96 * k + 96] = lax.dot_general(
            part, widen, (((1,), (1,)), ((), ())), precision=highest, preferred_element_type=f32
        )


def local_kernel(u, nodes, got):
    zero = jnp.zeros((8, LANES), f32)

    def block(i, carry):
        first = pl.multiple_of(8 * i, 8)
        index = [nodes[pl.ds(first, 8), LANES * t : LANES * t + LANES] for t in range(4)]
        high = [x >> 7 for x in index]
        low = [x & 127 for x in index]
        acc = gather_rows(
            lambda c, r: u[c, r : r + 1, :], 0, ROWS, high, low, [[zero] * 3 for t in range(4)]
        )
        for t in range(4):
            for c in range(3):
                got[c, pl.ds(first, 8), LANES * t : LANES * t + LANES] = acc[t][c]
        return carry

    lax.fori_loop(0, 4, block, 0)


def element_kernel(flags, got, nodes, moduli, stiff, uown, e, o, f, b, r_out, m_next, facing,
                   pay_e, pay_o, pay_f, pay_b, ghost, wide, out):
    sides = from_sides(flags, e, o, f, b)
    for k in range(4):
        for c in range(3):
            ghost[c, 2 * k : 2 * k + 2, :] = sides[k][2 * c : 2 * c + 2, :]
    m_next[...] = uown[...] - e[8:20, :]
    facing[...] = e[20:32, :]

    def block(i, carry):
        first = pl.multiple_of(8 * i, 8)
        lanes = [slice(LANES * t, LANES * t + LANES) for t in range(4)]
        index = [nodes[pl.ds(first, 8), lane] for lane in lanes]
        high = [x >> 7 for x in index]
        low = [x & 127 for x in index]
        acc = gather_rows(
            lambda c, r: ghost[c, r : r + 1, :], ROWS, 8, high, low,
            [[got[c, pl.ds(first, 8), lane] for c in range(3)] for lane in lanes],
        )
        for t in range(4):
            for c in range(3):
                for k in range(2):
                    row = pl.multiple_of(96 * k + 32 * c + 8 * i, 8)
                    wide[pl.ds(row, 8), lanes[t]] = acc[t][c] * moduli[k : k + 1, lanes[t]]
        return carry

    lax.fori_loop(0, 4, block, 0)
    r_out[...] = jnp.dot(stiff[...], wide[...], precision=highest, preferred_element_type=f32)

    def scatter(i, total):
        spreads, hots = [], []
        for n in range(3):
            a = 3 * i + n
            index = nodes[pl.ds(a, 1), :]
            values = [r_out[pl.ds(32 * c + a, 1), :] for c in range(3)]
            spreads.append(spread_ghost(index >> 8, values))
            hots.append(one_hot_low(index & 255))
        return total + times_one_hot(
            jnp.concatenate(spreads, axis=1), jnp.concatenate(hots, axis=1)
        )

    total = lax.fori_loop(0, 9, scatter, jnp.zeros((32, 256), f32))
    both = total[0:16] + total[16:32]
    out[...] = both
    odd = flags[0] == 1
    for dst in (pay_e, pay_o, pay_f, pay_b):
        dst[6:8, :] = jnp.zeros((2, LANES), f32)
    for c in range(3):
        for h in range(2):
            lane = slice(LANES * h, LANES * h + LANES)
            blocks = [out[4 * c + k : 4 * c + k + 1, lane] for k in range(4)]
            row = slice(2 * c + h, 2 * c + h + 1)
            pay_e[row, :] = jnp.where(odd, blocks[0], blocks[1])
            pay_o[row, :] = jnp.where(odd, blocks[1], blocks[0])
            pay_b[row, :] = blocks[2]
            pay_f[row, :] = blocks[3]


def owned_kernel(r, nodes, sf, m, facing, part):
    def scatter(i, total):
        spreads, hots = [], []
        for n in range(3):
            a = 3 * i + n
            index = nodes[pl.ds(a, 1), :]
            values = [r[pl.ds(32 * c + a, 1), :] for c in range(3)]
            spreads.append(spread_owned(index >> 8, values))
            hots.append(one_hot_low(index & 255))
        return total + times_one_hot(
            jnp.concatenate(spreads, axis=1), jnp.concatenate(hots, axis=1)
        )

    total = lax.fori_loop(0, 9, scatter, jnp.zeros((96, 256), f32))
    spreads, hots = [], []
    for t in range(8):
        index = sf[8 + t : 9 + t, :]
        if t < 4:
            values = [-facing[4 * c + t : 4 * c + t + 1, :] for c in range(3)]
        else:
            values = [m[4 * c + t - 4 : 4 * c + t - 3, :] for c in range(3)]
        spreads.append(spread_owned(index >> 8, values))
        hots.append(one_hot_low(index & 255))
    total += times_one_hot(jnp.concatenate(spreads, axis=1), jnp.concatenate(hots, axis=1))
    part[...] = total[0:48] + total[48:96]


def assemble(flags, part, sf, e, o, f, b, w):
    sides = from_sides(flags, e, o, f, b)
    spreads, hots = [], []
    for s in range(4):
        for h in range(2):
            index = sf[2 * s + h : 2 * s + h + 1, :]
            values = [sides[s][2 * c + h : 2 * c + h + 1, :] for c in range(3)]
            spreads.append(spread_owned(index >> 8, values))
            hots.append(one_hot_low(index & 255))
    total = times_one_hot(jnp.concatenate(spreads, axis=1), jnp.concatenate(hots, axis=1))
    total = part[...] + total[0:48] + total[48:96]
    for c in range(3):
        for h in range(2):
            w[c, pl.ds(h, 16, stride=2), :] = total[
                16 * c : 16 * c + 16, LANES * h : LANES * h + LANES
            ]


def next_kernel(flags, part, sf, m_next, inv, e, o, f, b, w, u, pay_e, pay_o, pay_f, pay_b, uown):
    assemble(flags, part, sf, e, o, f, b, w)
    apply_blocks(inv, w, u)
    send_payloads(flags[0], u, m_next[...], sf, pay_e, pay_o, pay_f, pay_b, uown)


def last_kernel(flags, part, sf, e, o, f, b, w0, w1, w2, m0, m1, m2, m3, w3, sums):
    assemble(flags, part, sf, e, o, f, b, w3)
    fields, mults = [w0, w1, w2, w3], [m0, m1, m2, m3]
    lane = lax.broadcasted_iota(i32, (1, LANES), 1)
    row = jnp.zeros((1, LANES), f32)
    place = 0
    for i in range(4):
        for j in range(i, 4):
            prod = fields[i][...] * fields[j][...]
            prod = jnp.sum(prod, axis=0)
            total = jnp.sum(prod, axis=0, keepdims=True) + jnp.sum(
                mults[i][...] * mults[j][...], axis=0, keepdims=True
            )
            row = jnp.where(lane == place, jnp.sum(total, axis=1, keepdims=True), row)
            place += 1
    sums[...] = jnp.broadcast_to(row[None], sums.shape)


def finish_kernel(sums, u0, u1, u2, m0, m1, m2, disp, mult, good):
    whole = jnp.sum(sums[:, 0, :], axis=0, keepdims=True)
    gram = {}
    place = 0
    for i in range(4):
        for j in range(i, 4):
            gram[i, j] = whole[0:1, place : place + 1]
            place += 1
    scale = [lax.rsqrt(gram[i, i]) for i in range(4)]
    scale = [s * (1.5 - 0.5 * ((gram[i, i] * s) * s)) for i, s in enumerate(scale)]
    norm = {(i, j): (gram[i, j] * scale[i]) * scale[j] for i, j in gram}
    d1 = norm[1, 1]
    l21 = norm[1, 2] / d1
    l31 = norm[1, 3] / d1
    d2 = norm[2, 2] - l21 * norm[1, 2]
    t32 = norm[2, 3] - l21 * norm[1, 3]
    l32 = t32 / d2
    d3 = norm[3, 3] - l31 * norm[1, 3] - l32 * t32
    z1 = norm[0, 1]
    z2 = norm[0, 2] - l21 * z1
    z3 = norm[0, 3] - l31 * z1 - l32 * z2
    y3 = z3 / d3
    y2 = z2 / d2 - l32 * y3
    y1 = z1 / d1 - l21 * y2 - l31 * y3
    root = gram[0, 0] * scale[0]
    coef = [y1 * (root * scale[1]), y2 * (root * scale[2]), y3 * (root * scale[3])]
    ok = (d2 > PIVOT_MIN) & (d3 > PIVOT_MIN)
    for i in range(4):
        ok = ok & (gram[i, i] > 1e-25) & (gram[i, i] < 1e37)
    good[...] = jnp.where(ok, 1, 0)
    fields, mults = [u0, u1, u2], [m0, m1, m2]
    for c in range(3):
        sol = coef[0] * u0[c] + coef[1] * u1[c] + coef[2] * u2[c]
        for r in range(ROWS):
            disp[c : c + 1, LANES * r : LANES * r + LANES] = sol[r : r + 1, :]
    sol = coef[0] * m0[...] + coef[1] * m1[...] + coef[2] * m2[...]
    for c in range(3):
        for t in range(4):
            mult[c : c + 1, LANES * t : LANES * t + LANES] = sol[4 * c + t : 4 * c + t + 1, :]


def exchange(pay_e, pay_o, pay_f, pay_b):
    count_x, count_y = lax.axis_size("px"), lax.axis_size("py")
    pairs = [(i, i ^ 1) for i in range(count_x)]
    others = [(i, (((i + 1) ^ 1) - 1) % count_x) for i in range(count_x)]
    forward = [(i, (i + 1) % count_y) for i in range(count_y)]
    backward = [(i, (i - 1) % count_y) for i in range(count_y)]
    return (
        lax.ppermute(pay_e, "px", pairs),
        lax.ppermute(pay_o, "px", others),
        lax.ppermute(pay_f, "py", forward),
        lax.ppermute(pay_b, "py", backward),
    )


def half_operator(flags, u, m, uown, pays, nodes, moduli, stiff, sf):
    came = exchange(*pays)
    (got,) = call(local_kernel, [shape(3, 32, 512)], [u, nodes], flops=20_000_000)
    r, m_next, facing, *pays = call(
        element_kernel,
        [shape(96, 512), shape(12, LANES), shape(12, LANES)] + [shape(8, LANES)] * 4,
        [flags, got, nodes, moduli, stiff, uown, *came],
        scratch=[
            pltpu.VMEM((3, 8, LANES), f32),
            pltpu.VMEM((192, 512), f32),
            pltpu.VMEM((16, 256), f32),
        ],
        smem_first=True,
    )
    back = exchange(*pays)
    (part,) = call(owned_kernel, [shape(48, 256)], [r, nodes, sf, m, facing], flops=20_000_000)
    return part, back, m_next


PAYLOADS = [shape(32, LANES), shape(8, LANES), shape(8, LANES), shape(8, LANES), shape(12, LANES)]


def least_squares(columns, beta):
    cosines, sines, upper = ([], [], [])
    target = [beta] + [jnp.zeros_like(beta) for later in columns]
    for position, column in enumerate(columns):
        column = list(column)
        for earlier in range(position):
            top = cosines[earlier] * column[earlier] + sines[earlier] * column[earlier + 1]
            below = -sines[earlier] * column[earlier] + cosines[earlier] * column[earlier + 1]
            column[earlier] = top
            column[earlier + 1] = below
        pivot = column[position]
        under = column[position + 1]
        radius = jnp.sqrt(pivot * pivot + under * under)
        cosine = pivot / radius
        sine = under / radius
        column[position] = radius
        cosines.append(cosine)
        sines.append(sine)
        target[position + 1] = -sine * target[position]
        target[position] = cosine * target[position]
        upper.append(column)
    count = len(columns)
    coeffs = [None] * count
    for row_index in reversed(range(count)):
        total = target[row_index]
        for later in range(row_index + 1, count):
            total = total - upper[later][row_index] * coeffs[later]
        coeffs[row_index] = total / upper[row_index][row_index]
    return coeffs


def inner(first, second):
    total = jnp.sum(first[0] * second[0]) + jnp.sum(first[1] * second[1])
    return lax.psum(total, ("px", "py"))


def apply_kernel(flags, w, m, inv, sf, u, pay_e, pay_o, pay_f, pay_b, uown):
    apply_blocks(inv, w, u)
    send_payloads(flags[0], u, m[...], sf, pay_e, pay_o, pay_f, pay_b, uown)


def step_by_step(flags, w0, m0, inv, nodes, moduli, stiff, sf):
    beta = jnp.sqrt(inner((w0, m0), (w0, m0)))
    basis_w = jnp.zeros((ITERS + 1,) + w0.shape, f32).at[0].set(w0 / beta)
    basis_m = jnp.zeros((ITERS + 1,) + m0.shape, f32).at[0].set(m0 / beta)
    solves = jnp.zeros((ITERS,) + w0.shape, f32)
    entries = jnp.zeros((ITERS, ITERS + 1), f32)

    def step(j, state):
        basis_w, basis_m, solves, entries = state
        m = basis_m[j]
        u, *pays, uown = call(
            apply_kernel, [shape(3, ROWS, LANES)] + PAYLOADS,
            [flags, basis_w[j], m, inv, sf], smem_first=True,
        )
        part, back, m_next = half_operator(flags, u, m, uown, pays, nodes, moduli, stiff, sf)
        w = call(
            next_kernel, [shape(3, ROWS, LANES)] * 2 + PAYLOADS,
            [flags, part, sf, m_next, inv, *back], smem_first=True,
        )[0]
        column = []
        for i in range(ITERS):
            entry = jnp.where(i <= j, inner((w, m_next), (basis_w[i], basis_m[i])), 0.0)
            w, m_next = w - entry * basis_w[i], m_next - entry * basis_m[i]
            column.append(entry)
        norm = jnp.sqrt(inner((w, m_next), (w, m_next)))
        column = jnp.stack(column + [jnp.zeros_like(norm)])
        column = jnp.where(jnp.arange(ITERS + 1) == j + 1, norm, column)
        return (
            basis_w.at[j + 1].set(w / norm),
            basis_m.at[j + 1].set(m_next / norm),
            solves.at[j].set(u),
            entries.at[j].set(column),
        )

    basis_w, basis_m, solves, entries = lax.fori_loop(
        0, ITERS, step, (basis_w, basis_m, solves, entries)
    )
    columns = [[entries[j, i] for i in range(j + 2)] for j in range(ITERS)]
    coeffs = least_squares(columns, beta)
    disp = sum(coeffs[j] * solves[j] for j in range(ITERS))
    mult = sum(coeffs[j] * basis_m[j] for j in range(ITERS))
    return disp.reshape(3, ROWS * LANES), mult.reshape(3, 4 * LANES)


def body(body_force, fault_slip, elem_nodes, moduli, stiff_ref, block_inv, send_nodes, fault_nodes):
    lame = moduli[0, 0]
    at_x, at_y = lax.axis_index("px"), lax.axis_index("py")
    count_x, count_y = lax.axis_size("px"), lax.axis_size("py")
    flags = jnp.stack(
        [at_x % 2, at_x > 0, at_x < count_x - 1, at_y > 0, at_y < count_y - 1]
    ).astype(i32)
    w0, m0, inv, u, sf, *pays, uown = call(
        first_kernel,
        [
            shape(3, ROWS, LANES), shape(12, LANES), shape(9, ROWS, LANES), shape(3, ROWS, LANES),
            jax.ShapeDtypeStruct((16, LANES), i32),
        ] + PAYLOADS,
        [flags, body_force[0, 0], fault_slip[0, 0], block_inv[0, 0], send_nodes[0, 0], fault_nodes[0, 0]],
        smem_first=True,
    )
    nodes, stiff = call(
        prepare_kernel,
        [jax.ShapeDtypeStruct((32, 512), i32), shape(96, 192)],
        [elem_nodes[0, 0], stiff_ref],
    )
    fields, mults, solves = [w0], [m0], []
    for j in range(ITERS):
        solves.append(u)
        part, back, m = half_operator(flags, u, mults[-1], uown, pays, nodes, lame, stiff, sf)
        mults.append(m)
        if j < ITERS - 1:
            w, u, *pays, uown = call(
                next_kernel, [shape(3, ROWS, LANES)] * 2 + PAYLOADS,
                [flags, part, sf, m, inv, *back], smem_first=True,
            )
            fields.append(w)
    count = count_x * count_y
    w, sums = call(
        last_kernel, [shape(3, ROWS, LANES), shape(count, 1, LANES)],
        [flags, part, sf, *back, *fields, *mults], smem_first=True,
    )
    sums = lax.all_to_all(sums, ("px", "py"), 0, 0)
    disp, mult, good = call(
        finish_kernel,
        [shape(3, ROWS * LANES), shape(3, 4 * LANES), jax.ShapeDtypeStruct((1, 1), i32)],
        [sums, *solves, *mults[:ITERS]],
    )
    disp, mult = lax.cond(
        good[0, 0] == 1,
        lambda: (disp, mult),
        lambda: step_by_step(flags, w0, m0, inv, nodes, lame, stiff, sf),
    )
    return (disp[None, None], mult[None, None])


def solution(mesh):
    split = P("px", "py", None, None)
    in_specs = (split, split, split, split, P(), split, split, split)
    return jax.shard_map(
        body, mesh=mesh, in_specs=in_specs, out_specs=(split, split), check_vma=False
    )
```

```python
import jax
import jax.numpy as jnp
from jax import lax
from jax.experimental import pallas as pl
from jax.experimental.pallas import tpu as pltpu
from jax.sharding import PartitionSpec as P

ITERS = 3
LANES = 128
ROWS = 32
PIVOT_MIN = 0.01
f32, bf16, i32, i16 = jnp.float32, jnp.bfloat16, jnp.int32, jnp.int16
highest = lax.Precision.HIGHEST

VMEM = pl.BlockSpec(memory_space=pltpu.VMEM)
SMEM = pl.BlockSpec(memory_space=pltpu.SMEM)


def shape(*dims):
    return jax.ShapeDtypeStruct(dims, f32)


def call(kernel, outs, args, scratch=(), smem_first=False, flops=2_000_000):
    specs = [VMEM] * len(args)
    if smem_first:
        specs[0] = SMEM
    return pl.pallas_call(
        kernel,
        out_shape=outs,
        in_specs=specs,
        out_specs=[VMEM] * len(outs),
        scratch_shapes=list(scratch),
        compiler_params=pltpu.CompilerParams(vmem_limit_bytes=32 * 1024 * 1024),
        cost_estimate=pl.CostEstimate(flops=flops, bytes_accessed=1_000_000, transcendentals=0),
    )(*args)


def take_lanes(row, lanes):
    return jnp.take_along_axis(
        jnp.broadcast_to(row, lanes.shape), lanes, axis=1, mode="promise_in_bounds"
    )


def gather_rows(table, first, count, high, low, start):
    acc = [list(per) for per in start]
    for r in range(count):
        rows = [table(c, r) for c in range(3)]
        for n in range(len(high)):
            here = high[n] == r + first
            for c in range(3):
                acc[n][c] = jnp.where(here, take_lanes(rows[c], low[n]), acc[n][c])
    return acc


def pair_rows(row):
    return jnp.broadcast_to(row, (16, row.shape[1]))


def one_hot_low(low_row):
    width = low_row.shape[1]
    low = pair_rows(low_row).astype(i16)
    rows = lax.broadcasted_iota(i16, (16, width), 0)
    one, zero = jnp.ones((16, width), bf16), jnp.zeros((16, width), bf16)
    return [jnp.where(rows + i16(16 * g) == low, one, zero) for g in range(16)]


def spread(high_row, values, with_ghost):
    width = high_row.shape[1]
    high = pair_rows(high_row).astype(i16)
    rows = lax.broadcasted_iota(i16, (16, width), 0)
    here = rows == high
    zero = jnp.zeros((16, width), bf16)
    wide = [pair_rows(value) for value in values]
    tops = [value.astype(bf16) for value in wide]
    lows = [(value - top.astype(f32)).astype(bf16) for value, top in zip(wide, tops)]
    parts = [jnp.where(here, value, zero) for value in tops + lows]
    if with_ghost:
        ghost = jnp.where(rows < 12, (rows & 3) + i16(16), i16(-1)) == high
        for v in (tops, lows):
            whole = jnp.where(rows < 4, v[0], jnp.where(rows < 8, v[1], v[2]))
            parts.append(jnp.where(ghost, whole, zero))
    return parts


def place_chunk(spreads, hots, chunk, index_row, values, with_ghost):
    lanes = slice(LANES * chunk, LANES * chunk + LANES)
    for g, part in enumerate(spread(index_row >> 8, values, with_ghost)):
        spreads[16 * g : 16 * g + 16, lanes] = part
    for g, part in enumerate(one_hot_low(index_row & 255)):
        hots[16 * g : 16 * g + 16, lanes] = part


def scatter_product(spreads, hots):
    return lax.dot_general(
        hots[...], spreads[...], (((1,), (1,)), ((), ())), preferred_element_type=f32
    ).T


def send_payloads(par, u_ref, m_rows, sf, pay_e, pay_o, pay_f, pay_b, uown):
    index = [sf[0:8, :], sf[8:16, :]]
    high = [x >> 7 for x in index]
    low = [x & 127 for x in index]
    zero = jnp.zeros((8, LANES), f32)
    got = gather_rows(
        lambda c, r: u_ref[c, r : r + 1, :], 0, ROWS, high, low, [[zero] * 3, [zero] * 3]
    )
    pad = jnp.zeros((2, LANES), f32)
    sides = [
        jnp.concatenate([got[0][c][2 * s : 2 * s + 2, :] for c in range(3)] + [pad], axis=0)
        for s in range(4)
    ]
    odd = par == 1
    pay_e[0:8, :] = jnp.where(odd, sides[0], sides[1])
    pay_o[...] = jnp.where(odd, sides[1], sides[0])
    pay_b[...] = sides[2]
    pay_f[...] = sides[3]
    for c in range(3):
        uown[4 * c : 4 * c + 4, :] = got[1][c][0:4, :]
        pay_e[8 + 4 * c : 12 + 4 * c, :] = got[1][c][4:8, :]
    pay_e[20:32, :] = m_rows


def apply_blocks(inv_ref, w_ref, u_ref):
    w = [w_ref[c] for c in range(3)]
    for i in range(3):
        u_ref[i] = inv_ref[3 * i] * w[0] + inv_ref[3 * i + 1] * w[1] + inv_ref[3 * i + 2] * w[2]


def from_sides(flags, e, o, f, b):
    odd = flags[0] == 1
    zero = jnp.zeros((8, LANES), f32)
    e, o = e[0:8, :], o[...]
    return [
        jnp.where(flags[1] == 1, jnp.where(odd, e, o), zero),
        jnp.where(flags[2] == 1, jnp.where(odd, o, e), zero),
        jnp.where(flags[3] == 1, f[...], zero),
        jnp.where(flags[4] == 1, b[...], zero),
    ]


def first_kernel(flags, w, slip, inv, send, fault, m, u, sf, pay_e, pay_o, pay_f, pay_b, uown):
    for c in range(3):
        m[4 * c : 4 * c + 4, :] = slip[c]
    for s in range(4):
        for h in range(2):
            sf[2 * s + h : 2 * s + h + 1, :] = send[s : s + 1, LANES * h : LANES * h + LANES]
    for k in range(2):
        for t in range(4):
            row = 8 + 4 * k + t
            sf[row : row + 1, :] = fault[k : k + 1, LANES * t : LANES * t + LANES]
    apply_blocks(inv, w, u)
    send_payloads(flags[0], u, m[...], sf, pay_e, pay_o, pay_f, pay_b, uown)


def prepare_kernel(nodes, stiff, nodes_out, stiff_out):
    for a in range(27):
        nodes_out[4 * a : 4 * a + 4, :] = nodes[a]
    nodes_out[108:112, :] = jnp.zeros((4, LANES), i32)
    rows = lax.broadcasted_iota(i32, (96, 81), 0)
    cols = lax.broadcasted_iota(i32, (96, 81), 1)
    a = rows & 31
    widen = jnp.where(((rows >> 5) * 27 + a == cols) & (a < 27), 1.0, 0.0)
    for k in range(2):
        part = jnp.dot(widen, stiff[:, k, :], precision=highest, preferred_element_type=f32)
        part = lax.dot_general(
            part, widen, (((1,), (1,)), ((), ())), precision=highest, preferred_element_type=f32
        )
        top = part.astype(bf16)
        low = (part - top.astype(f32)).astype(bf16)
        stiff_out[96 * k : 96 * k + 96, :] = jnp.concatenate([top, top, low], axis=1)


def local_kernel(u, nodes, got):
    zero = jnp.zeros((8, LANES), f32)
    for i in range(14):
        index = nodes[8 * i : 8 * i + 8, :]
        (acc,) = gather_rows(
            lambda c, r: u[c, r : r + 1, :], 0, ROWS, [index >> 7], [index & 127], [[zero] * 3]
        )
        for c in range(3):
            got[c, 8 * i : 8 * i + 8, :] = acc[c]


def element_kernel(flags, got, nodes, moduli, stiff, sf, m, uown, e, o, f, b,
                   part, m_next, pay_e, pay_o, pay_f, pay_b, ghost, full, wide, r, spreads, hots, out):
    sides = from_sides(flags, e, o, f, b)
    for k in range(4):
        for c in range(3):
            ghost[c, 2 * k : 2 * k + 2, :] = sides[k][2 * c : 2 * c + 2, :]
    m_next[...] = uown[...] - e[8:20, :]
    for i in range(14):
        rows = slice(8 * i, 8 * i + 8)
        index = nodes[rows, :]
        (acc,) = gather_rows(
            lambda c, r: ghost[c, r : r + 1, :], ROWS, 8, [index >> 7], [index & 127],
            [[got[c, rows, :] for c in range(3)]],
        )
        for c in range(3):
            full[c, rows, :] = acc[c]
    for c in range(3):
        wide[32 * c + 24 : 32 * c + 32, :] = jnp.zeros((8, 512), f32)
        for t in range(4):
            wide[32 * c : 32 * c + 27, LANES * t : LANES * t + LANES] = full[
                c, pl.ds(t, 27, stride=4), :
            ]
    local = wide[...]
    top = local.astype(bf16)
    low = (local - top.astype(f32)).astype(bf16)
    both = jnp.dot(
        stiff[...], jnp.concatenate([top, low, top], axis=0), preferred_element_type=f32
    )
    r[...] = both[0:96] * moduli[0:1, :] + both[96:192] * moduli[1:2, :]
    for a in range(27):
        for t in range(4):
            lanes = slice(LANES * t, LANES * t + LANES)
            row = 4 * a + t
            values = [r[32 * c + a : 32 * c + a + 1, lanes] for c in range(3)]
            place_chunk(spreads, hots, row, nodes[row : row + 1, :], values, True)
    for t in range(8):
        if t < 4:
            values = [m[4 * c + t : 4 * c + t + 1, :] for c in range(3)]
        else:
            values = [-e[16 + 4 * c + t : 17 + 4 * c + t, :] for c in range(3)]
        place_chunk(spreads, hots, 108 + t, sf[8 + t : 9 + t, :], values, True)
    total = scatter_product(spreads, hots)
    part[...] = total[0:48] + total[48:96]
    out[...] = total[96:112] + total[112:128]
    odd = flags[0] == 1
    for dst in (pay_e, pay_o, pay_f, pay_b):
        dst[6:8, :] = jnp.zeros((2, LANES), f32)
    for c in range(3):
        for h in range(2):
            lane = slice(LANES * h, LANES * h + LANES)
            blocks = [out[4 * c + k : 4 * c + k + 1, lane] for k in range(4)]
            row = slice(2 * c + h, 2 * c + h + 1)
            pay_e[row, :] = jnp.where(odd, blocks[0], blocks[1])
            pay_o[row, :] = jnp.where(odd, blocks[1], blocks[0])
            pay_b[row, :] = blocks[2]
            pay_f[row, :] = blocks[3]


def assemble(flags, part, sf, e, o, f, b, w, spreads, hots):
    sides = from_sides(flags, e, o, f, b)
    for s in range(4):
        for h in range(2):
            row = 2 * s + h
            values = [sides[s][2 * c + h : 2 * c + h + 1, :] for c in range(3)]
            place_chunk(spreads, hots, row, sf[row : row + 1, :], values, False)
    total = scatter_product(spreads, hots)
    total = part[...] + total[0:48] + total[48:96]
    for c in range(3):
        for h in range(2):
            w[c, pl.ds(h, 16, stride=2), :] = total[
                16 * c : 16 * c + 16, LANES * h : LANES * h + LANES
            ]


def next_kernel(flags, part, sf, m_next, inv, e, o, f, b, w, u, pay_e, pay_o, pay_f, pay_b, uown,
                spreads, hots):
    assemble(flags, part, sf, e, o, f, b, w, spreads, hots)
    apply_blocks(inv, w, u)
    send_payloads(flags[0], u, m_next[...], sf, pay_e, pay_o, pay_f, pay_b, uown)


def last_kernel(flags, part, sf, e, o, f, b, w0, w1, w2, m0, m1, m2, m3, sums, w3, spreads, hots):
    assemble(flags, part, sf, e, o, f, b, w3, spreads, hots)
    fields, mults = [w0, w1, w2, w3], [m0, m1, m2, m3]
    lane = lax.broadcasted_iota(i32, (1, LANES), 1)
    row = jnp.zeros((1, LANES), f32)
    place = 0
    for i in range(4):
        for j in range(i, 4):
            prod = fields[i][...] * fields[j][...]
            prod = jnp.sum(prod, axis=0)
            total = jnp.sum(prod, axis=0, keepdims=True) + jnp.sum(
                mults[i][...] * mults[j][...], axis=0, keepdims=True
            )
            row = jnp.where(lane == place, jnp.sum(total, axis=1, keepdims=True), row)
            place += 1
    sums[...] = row


def solve_kernel(sums, coeffs, good):
    whole = jnp.sum(sums[:, 0, :], axis=0, keepdims=True)
    gram = {}
    place = 0
    for i in range(4):
        for j in range(i, 4):
            gram[i, j] = whole[0:1, place : place + 1]
            place += 1
    scale = [lax.rsqrt(gram[i, i]) for i in range(4)]
    scale = [s * (1.5 - 0.5 * ((gram[i, i] * s) * s)) for i, s in enumerate(scale)]
    norm = {(i, j): (gram[i, j] * scale[i]) * scale[j] for i, j in gram}
    d1 = norm[1, 1]
    l21 = norm[1, 2] / d1
    l31 = norm[1, 3] / d1
    d2 = norm[2, 2] - l21 * norm[1, 2]
    t32 = norm[2, 3] - l21 * norm[1, 3]
    l32 = t32 / d2
    d3 = norm[3, 3] - l31 * norm[1, 3] - l32 * t32
    z1 = norm[0, 1]
    z2 = norm[0, 2] - l21 * z1
    z3 = norm[0, 3] - l31 * z1 - l32 * z2
    y3 = z3 / d3
    y2 = z2 / d2 - l32 * y3
    y1 = z1 / d1 - l21 * y2 - l31 * y3
    root = gram[0, 0] * scale[0]
    coef = [y1 * (root * scale[1]), y2 * (root * scale[2]), y3 * (root * scale[3])]
    ok = (d2 > PIVOT_MIN) & (d3 > PIVOT_MIN)
    for i in range(4):
        ok = ok & (gram[i, i] > 1e-25) & (gram[i, i] < 1e37)
    good[...] = jnp.where(ok, 1, 0)
    lane = lax.broadcasted_iota(i32, (8, LANES), 0)
    coeffs[...] = jnp.where(lane == 0, coef[0], jnp.where(lane == 1, coef[1], coef[2]))


def finish_kernel(coeffs, u0, u1, u2, m0, m1, m2, disp, mult):
    coef = [coeffs[j : j + 1, :] for j in range(ITERS)]
    for c in range(3):
        disp[c] = coef[0] * u0[c] + coef[1] * u1[c] + coef[2] * u2[c]
        rows = slice(4 * c, 4 * c + 4)
        mult[c] = coef[0] * m0[rows, :] + coef[1] * m1[rows, :] + coef[2] * m2[rows, :]


def exchange(pay_e, pay_o, pay_f, pay_b):
    count_x, count_y = lax.axis_size("px"), lax.axis_size("py")
    pairs = [(i, i ^ 1) for i in range(count_x)]
    others = [(i, (((i + 1) ^ 1) - 1) % count_x) for i in range(count_x)]
    forward = [(i, (i + 1) % count_y) for i in range(count_y)]
    backward = [(i, (i - 1) % count_y) for i in range(count_y)]
    return (
        lax.ppermute(pay_e, "px", pairs),
        lax.ppermute(pay_o, "px", others),
        lax.ppermute(pay_f, "py", forward),
        lax.ppermute(pay_b, "py", backward),
    )


def half_operator(flags, u, m, uown, pays, nodes, moduli, stiff, sf):
    came = exchange(*pays)
    (got,) = call(local_kernel, [shape(3, 112, LANES)], [u, nodes], flops=20_000_000)
    part, m_next, *pays = call(
        element_kernel,
        [shape(48, 256), shape(12, LANES)] + [shape(8, LANES)] * 4,
        [flags, got, nodes, moduli, stiff, sf, m, uown, *came],
        scratch=[
            pltpu.VMEM((3, 8, LANES), f32),
            pltpu.VMEM((3, 112, LANES), f32),
            pltpu.VMEM((96, 512), f32),
            pltpu.VMEM((96, 512), f32),
            pltpu.VMEM((128, 116 * LANES), bf16),
            pltpu.VMEM((256, 116 * LANES), bf16),
            pltpu.VMEM((16, 256), f32),
        ],
        smem_first=True,
    )
    return part, exchange(*pays), m_next


SMALL = [pltpu.VMEM((96, 8 * LANES), bf16), pltpu.VMEM((256, 8 * LANES), bf16)]
PAYLOADS = [shape(32, LANES), shape(8, LANES), shape(8, LANES), shape(8, LANES), shape(12, LANES)]


def least_squares(columns, beta):
    cosines, sines, upper = ([], [], [])
    target = [beta] + [jnp.zeros_like(beta) for later in columns]
    for position, column in enumerate(columns):
        column = list(column)
        for earlier in range(position):
            top = cosines[earlier] * column[earlier] + sines[earlier] * column[earlier + 1]
            below = -sines[earlier] * column[earlier] + cosines[earlier] * column[earlier + 1]
            column[earlier] = top
            column[earlier + 1] = below
        pivot = column[position]
        under = column[position + 1]
        radius = jnp.sqrt(pivot * pivot + under * under)
        cosine = pivot / radius
        sine = under / radius
        column[position] = radius
        cosines.append(cosine)
        sines.append(sine)
        target[position + 1] = -sine * target[position]
        target[position] = cosine * target[position]
        upper.append(column)
    count = len(columns)
    coeffs = [None] * count
    for row_index in reversed(range(count)):
        total = target[row_index]
        for later in range(row_index + 1, count):
            total = total - upper[later][row_index] * coeffs[later]
        coeffs[row_index] = total / upper[row_index][row_index]
    return coeffs


def inner(first, second):
    total = jnp.sum(first[0] * second[0]) + jnp.sum(first[1] * second[1])
    return lax.psum(total, ("px", "py"))


def apply_kernel(flags, w, m, inv, sf, u, pay_e, pay_o, pay_f, pay_b, uown):
    apply_blocks(inv, w, u)
    send_payloads(flags[0], u, m[...], sf, pay_e, pay_o, pay_f, pay_b, uown)


def step_by_step(flags, w0, m0, inv, nodes, moduli, stiff, sf):
    beta = jnp.sqrt(inner((w0, m0), (w0, m0)))
    basis_w = jnp.zeros((ITERS + 1,) + w0.shape, f32).at[0].set(w0 / beta)
    basis_m = jnp.zeros((ITERS + 1,) + m0.shape, f32).at[0].set(m0 / beta)
    solves = jnp.zeros((ITERS,) + w0.shape, f32)
    entries = jnp.zeros((ITERS, ITERS + 1), f32)

    def step(j, state):
        basis_w, basis_m, solves, entries = state
        m = basis_m[j]
        u, *pays, uown = call(
            apply_kernel, [shape(3, ROWS, LANES)] + PAYLOADS,
            [flags, basis_w[j], m, inv, sf], smem_first=True,
        )
        part, back, m_next = half_operator(flags, u, m, uown, pays, nodes, moduli, stiff, sf)
        w = call(
            next_kernel, [shape(3, ROWS, LANES)] * 2 + PAYLOADS,
            [flags, part, sf, m_next, inv, *back], scratch=SMALL, smem_first=True,
        )[0]
        column = []
        for i in range(ITERS):
            entry = jnp.where(i <= j, inner((w, m_next), (basis_w[i], basis_m[i])), 0.0)
            w, m_next = w - entry * basis_w[i], m_next - entry * basis_m[i]
            column.append(entry)
        norm = jnp.sqrt(inner((w, m_next), (w, m_next)))
        column = jnp.stack(column + [jnp.zeros_like(norm)])
        column = jnp.where(jnp.arange(ITERS + 1) == j + 1, norm, column)
        return (
            basis_w.at[j + 1].set(w / norm),
            basis_m.at[j + 1].set(m_next / norm),
            solves.at[j].set(u),
            entries.at[j].set(column),
        )

    basis_w, basis_m, solves, entries = lax.fori_loop(
        0, ITERS, step, (basis_w, basis_m, solves, entries)
    )
    columns = [[entries[j, i] for i in range(j + 2)] for j in range(ITERS)]
    coeffs = least_squares(columns, beta)
    disp = sum(coeffs[j] * solves[j] for j in range(ITERS))
    mult = sum(coeffs[j] * basis_m[j] for j in range(ITERS))
    return disp, mult.reshape(3, 4, LANES)


def body(body_force, fault_slip, elem_nodes, moduli, stiff_ref, block_inv, send_nodes, fault_nodes):
    lame = moduli[0, 0]
    at_x, at_y = lax.axis_index("px"), lax.axis_index("py")
    count_x, count_y = lax.axis_size("px"), lax.axis_size("py")
    flags = jnp.stack(
        [at_x % 2, at_x > 0, at_x < count_x - 1, at_y > 0, at_y < count_y - 1]
    ).astype(i32)
    w0 = body_force.reshape(3, ROWS, LANES)
    inv = block_inv.reshape(9, ROWS, LANES)
    m0, u, sf, *pays, uown = call(
        first_kernel,
        [shape(12, LANES), shape(3, ROWS, LANES), jax.ShapeDtypeStruct((16, LANES), i32)] + PAYLOADS,
        [flags, w0, fault_slip.reshape(3, 4, LANES), inv, send_nodes[0, 0], fault_nodes[0, 0]],
        smem_first=True,
    )
    nodes, stiff = call(
        prepare_kernel,
        [jax.ShapeDtypeStruct((112, LANES), i32), jax.ShapeDtypeStruct((192, 288), bf16)],
        [elem_nodes.reshape(27, 4, LANES), stiff_ref.transpose(1, 0, 2)],
    )
    fields, mults, solves = [w0], [m0], []
    for j in range(ITERS):
        solves.append(u)
        part, back, m = half_operator(flags, u, mults[-1], uown, pays, nodes, lame, stiff, sf)
        mults.append(m)
        if j < ITERS - 1:
            w, u, *pays, uown = call(
                next_kernel, [shape(3, ROWS, LANES)] * 2 + PAYLOADS,
                [flags, part, sf, m, inv, *back], scratch=SMALL, smem_first=True,
            )
            fields.append(w)
    count = count_x * count_y
    (sums,) = call(
        last_kernel, [shape(1, LANES)], [flags, part, sf, *back, *fields, *mults],
        scratch=[pltpu.VMEM((3, ROWS, LANES), f32)] + SMALL, smem_first=True,
    )
    sums = lax.all_to_all(
        jnp.broadcast_to(sums[None], (count, 1, LANES)), ("px", "py"), 0, 0
    )
    coeffs, good = call(
        solve_kernel, [shape(8, LANES), jax.ShapeDtypeStruct((1, 1), i32)], [sums]
    )
    disp, mult = lax.cond(
        good[0, 0] == 1,
        lambda: tuple(
            call(
                finish_kernel,
                [shape(3, ROWS, LANES), shape(3, 4, LANES)],
                [coeffs, *solves, *mults[:ITERS]],
            )
        ),
        lambda: step_by_step(flags, w0, m0, inv, nodes, lame, stiff, sf),
    )
    return (disp.reshape(body_force.shape), mult.reshape(fault_slip.shape))


def solution(mesh):
    split = P("px", "py", None, None)
    in_specs = (split, split, split, split, P(), split, split, split)
    return jax.shard_map(
        body, mesh=mesh, in_specs=in_specs, out_specs=(split, split), check_vma=False
    )
```

```python
import jax
import jax.numpy as jnp
from jax import lax
from jax.experimental import pallas as pl
from jax.experimental.pallas import tpu as pltpu
from jax.sharding import PartitionSpec as P

ITERS = 3
LANES = 128
ROWS = 32
PIVOT_MIN = 0.01
LARGE = 54
f32, bf16, i32, i16 = jnp.float32, jnp.bfloat16, jnp.int32, jnp.int16
highest = lax.Precision.HIGHEST

VMEM = pl.BlockSpec(memory_space=pltpu.VMEM)
SMEM = pl.BlockSpec(memory_space=pltpu.SMEM)


def shape(*dims):
    return jax.ShapeDtypeStruct(dims, f32)


def call(kernel, outs, args, scratch=(), smem_first=False, flops=2_000_000, grant=24):
    specs = [VMEM] * len(args)
    if smem_first:
        specs[0] = SMEM
    return pl.pallas_call(
        kernel,
        out_shape=outs,
        in_specs=specs,
        out_specs=[VMEM] * len(outs),
        scratch_shapes=list(scratch),
        compiler_params=pltpu.CompilerParams(vmem_limit_bytes=grant * 1024 * 1024),
        cost_estimate=pl.CostEstimate(flops=flops, bytes_accessed=1_000_000, transcendentals=0),
    )(*args)


def take_lanes(row, lanes):
    return jnp.take_along_axis(
        jnp.broadcast_to(row, lanes.shape), lanes, axis=1, mode="promise_in_bounds"
    )


def gather_rows(table, first, count, high, low, start):
    acc = [list(per) for per in start]
    for r in range(count):
        rows = [table(c, r) for c in range(3)]
        for n in range(len(high)):
            here = high[n] == r + first
            for c in range(3):
                acc[n][c] = jnp.where(here, take_lanes(rows[c], low[n]), acc[n][c])
    return acc


def pair_rows(row):
    return jnp.broadcast_to(row, (16, row.shape[1]))


def one_hot_low(low_row):
    width = low_row.shape[1]
    low = pair_rows(low_row).astype(i16)
    rows = lax.broadcasted_iota(i16, (16, width), 0)
    one, zero = jnp.ones((16, width), bf16), jnp.zeros((16, width), bf16)
    return [jnp.where(rows + i16(16 * g) == low, one, zero) for g in range(16)]


def spread(high_row, values, with_ghost):
    width = high_row.shape[1]
    high = pair_rows(high_row).astype(i16)
    rows = lax.broadcasted_iota(i16, (16, width), 0)
    here = rows == high
    zero = jnp.zeros((16, width), bf16)
    wide = [pair_rows(value) for value in values]
    tops = [value.astype(bf16) for value in wide]
    lows = [(value - top.astype(f32)).astype(bf16) for value, top in zip(wide, tops)]
    parts = [jnp.where(here, value, zero) for value in tops + lows]
    if with_ghost:
        ghost = jnp.where(rows < 12, (rows & 3) + i16(16), i16(-1)) == high
        for v in (tops, lows):
            whole = jnp.where(rows < 4, v[0], jnp.where(rows < 8, v[1], v[2]))
            parts.append(jnp.where(ghost, whole, zero))
    return parts


def place_chunk(spreads, hots, chunk, index_row, values, with_ghost):
    lanes = slice(LANES * chunk, LANES * chunk + LANES)
    for g, part in enumerate(spread(index_row >> 8, values, with_ghost)):
        spreads[16 * g : 16 * g + 16, lanes] = part
    if hots is None:
        return
    for g, part in enumerate(one_hot_low(index_row & 255)):
        hots[16 * g : 16 * g + 16, lanes] = part


def scatter_product(spreads, hots):
    return lax.dot_general(
        hots[...], spreads[...], (((1,), (1,)), ((), ())), preferred_element_type=f32
    ).T


def send_payloads(par, u_ref, m_rows, sf, pay_e, pay_o, pay_f, pay_b, uown):
    index = [sf[0:8, :], sf[8:16, :]]
    high = [x >> 7 for x in index]
    low = [x & 127 for x in index]
    zero = jnp.zeros((8, LANES), f32)
    got = gather_rows(
        lambda c, r: u_ref[c, r : r + 1, :], 0, ROWS, high, low, [[zero] * 3, [zero] * 3]
    )
    pad = jnp.zeros((2, LANES), f32)
    sides = [
        jnp.concatenate([got[0][c][2 * s : 2 * s + 2, :] for c in range(3)] + [pad], axis=0)
        for s in range(4)
    ]
    odd = par == 1
    pay_e[0:8, :] = jnp.where(odd, sides[0], sides[1])
    pay_o[...] = jnp.where(odd, sides[1], sides[0])
    pay_b[...] = sides[2]
    pay_f[...] = sides[3]
    for c in range(3):
        uown[4 * c : 4 * c + 4, :] = got[1][c][0:4, :]
        pay_e[8 + 4 * c : 12 + 4 * c, :] = got[1][c][4:8, :]
    pay_e[20:32, :] = m_rows


def apply_blocks(inv_ref, w_ref, u_ref):
    w = [w_ref[c] for c in range(3)]
    for i in range(3):
        u_ref[i] = inv_ref[3 * i] * w[0] + inv_ref[3 * i + 1] * w[1] + inv_ref[3 * i + 2] * w[2]


def from_sides(flags, e, o, f, b):
    odd = flags[0] == 1
    zero = jnp.zeros((8, LANES), f32)
    e, o = e[0:8, :], o[...]
    return [
        jnp.where(flags[1] == 1, jnp.where(odd, e, o), zero),
        jnp.where(flags[2] == 1, jnp.where(odd, o, e), zero),
        jnp.where(flags[3] == 1, f[...], zero),
        jnp.where(flags[4] == 1, b[...], zero),
    ]


def first_kernel(flags, w, slip, inv, send, fault, m, u, sf, pay_e, pay_o, pay_f, pay_b, uown):
    for c in range(3):
        m[4 * c : 4 * c + 4, :] = slip[c]
    for s in range(4):
        for h in range(2):
            sf[2 * s + h : 2 * s + h + 1, :] = send[s : s + 1, LANES * h : LANES * h + LANES]
    for k in range(2):
        for t in range(4):
            row = 8 + 4 * k + t
            sf[row : row + 1, :] = fault[k : k + 1, LANES * t : LANES * t + LANES]
    apply_blocks(inv, w, u)
    send_payloads(flags[0], u, m[...], sf, pay_e, pay_o, pay_f, pay_b, uown)


def prepare_kernel(nodes, stiff, moduli, nodes_out, stiff_out, moduli_out):
    moduli_out[...] = moduli[...]
    for a in range(27):
        nodes_out[4 * a : 4 * a + 4, :] = nodes[a]
    nodes_out[108:112, :] = jnp.zeros((4, LANES), i32)
    rows = lax.broadcasted_iota(i32, (96, 81), 0)
    cols = lax.broadcasted_iota(i32, (96, 81), 1)
    a = rows & 31
    widen = jnp.where(((rows >> 5) * 27 + a == cols) & (a < 27), 1.0, 0.0)
    for k in range(2):
        part = jnp.dot(widen, stiff[:, k, :], precision=highest, preferred_element_type=f32)
        part = lax.dot_general(
            part, widen, (((1,), (1,)), ((), ())), precision=highest, preferred_element_type=f32
        )
        top = part.astype(bf16)
        low = (part - top.astype(f32)).astype(bf16)
        stiff_out[96 * k : 96 * k + 96, :] = jnp.concatenate([top, top, low], axis=1)


def local_kernel(u, nodes, got):
    zero = jnp.zeros((8, LANES), f32)
    for i in range(14):
        index = nodes[8 * i : 8 * i + 8, :]
        (acc,) = gather_rows(
            lambda c, r: u[c, r : r + 1, :], 0, ROWS, [index >> 7], [index & 127], [[zero] * 3]
        )
        for c in range(3):
            got[c, 8 * i : 8 * i + 8, :] = acc[c]


def columns_kernel(nodes, sf, after, hots, send_hots):
    low = jnp.concatenate(
        [nodes[0:108, :], sf[8:16, :], sf[0:8, :], jnp.zeros((4, LANES), i32)], axis=0
    )
    low = (low & 255).astype(f32).T
    lanes = lax.broadcasted_iota(i32, (LANES, 256), 1).astype(f32)
    for chunk in range(124):
        column = jnp.broadcast_to(low[:, chunk : chunk + 1], (LANES, 256))
        made = jnp.where(lanes == column, 1.0, 0.0).astype(bf16)
        dst, place = (hots, chunk) if chunk < 116 else (send_hots, chunk - 116)
        dst[LANES * place : LANES * place + LANES, :] = made


def late_element_kernel(flags, got, nodes, moduli, stiff, sf, m, uown, e, o, f, b, columns,
                        part, m_next, pay_e, pay_o, pay_f, pay_b, ghost, full, wide, r, spreads, out):
    element_kernel(
        flags, got, nodes, moduli, stiff, sf, m, uown, e, o, f, b,
        part, m_next, pay_e, pay_o, pay_f, pay_b, ghost, full, wide, r, spreads, None, out, columns,
    )


def element_kernel(flags, got, nodes, moduli, stiff, sf, m, uown, e, o, f, b,
                   part, m_next, pay_e, pay_o, pay_f, pay_b, ghost, full, wide, r, spreads, hots, out,
                   columns=None):
    sides = from_sides(flags, e, o, f, b)
    for k in range(4):
        for c in range(3):
            ghost[c, 2 * k : 2 * k + 2, :] = sides[k][2 * c : 2 * c + 2, :]
    m_next[...] = uown[...] - e[8:20, :]
    for i in range(14):
        rows = slice(8 * i, 8 * i + 8)
        index = nodes[rows, :]
        (acc,) = gather_rows(
            lambda c, r: ghost[c, r : r + 1, :], ROWS, 8, [index >> 7], [index & 127],
            [[got[c, rows, :] for c in range(3)]],
        )
        for c in range(3):
            full[c, rows, :] = acc[c]
    for c in range(3):
        wide[32 * c + 24 : 32 * c + 32, :] = jnp.zeros((8, 512), f32)
        for t in range(4):
            wide[32 * c : 32 * c + 27, LANES * t : LANES * t + LANES] = full[
                c, pl.ds(t, 27, stride=4), :
            ]
    local = wide[...]
    top = local.astype(bf16)
    low = (local - top.astype(f32)).astype(bf16)
    both = jnp.dot(
        stiff[...], jnp.concatenate([top, low, top], axis=0), preferred_element_type=f32
    )
    r[...] = both[0:96] * moduli[0:1, :] + both[96:192] * moduli[1:2, :]
    for a in range(27):
        for t in range(4):
            lanes = slice(LANES * t, LANES * t + LANES)
            row = 4 * a + t
            values = [r[32 * c + a : 32 * c + a + 1, lanes] for c in range(3)]
            place_chunk(spreads, hots, row, nodes[row : row + 1, :], values, True)
    for t in range(8):
        if t < 4:
            values = [m[4 * c + t : 4 * c + t + 1, :] for c in range(3)]
        else:
            values = [-e[16 + 4 * c + t : 17 + 4 * c + t, :] for c in range(3)]
        place_chunk(spreads, hots, 108 + t, sf[8 + t : 9 + t, :], values, True)
    if columns is None:
        total = scatter_product(spreads, hots)
    else:
        total = jnp.dot(spreads[...], columns[...], preferred_element_type=f32)
    part[...] = total[0:48] + total[48:96]
    out[...] = total[96:112] + total[112:128]
    odd = flags[0] == 1
    for dst in (pay_e, pay_o, pay_f, pay_b):
        dst[6:8, :] = jnp.zeros((2, LANES), f32)
    for c in range(3):
        for h in range(2):
            lane = slice(LANES * h, LANES * h + LANES)
            blocks = [out[4 * c + k : 4 * c + k + 1, lane] for k in range(4)]
            row = slice(2 * c + h, 2 * c + h + 1)
            pay_e[row, :] = jnp.where(odd, blocks[0], blocks[1])
            pay_o[row, :] = jnp.where(odd, blocks[1], blocks[0])
            pay_b[row, :] = blocks[2]
            pay_f[row, :] = blocks[3]


def assemble(flags, part, sf, e, o, f, b, w, spreads, hots, send_columns):
    sides = from_sides(flags, e, o, f, b)
    for s in range(4):
        for h in range(2):
            row = 2 * s + h
            values = [sides[s][2 * c + h : 2 * c + h + 1, :] for c in range(3)]
            place_chunk(spreads, hots, row, sf[row : row + 1, :], values, False)
    if send_columns is None:
        total = scatter_product(spreads, hots)
    else:
        total = jnp.dot(spreads[...], send_columns[...], preferred_element_type=f32)
    total = part[...] + total[0:48] + total[48:96]
    for c in range(3):
        for h in range(2):
            w[c, pl.ds(h, 16, stride=2), :] = total[
                16 * c : 16 * c + 16, LANES * h : LANES * h + LANES
            ]


def alone_kernel(flags, part, sf, e, o, f, b, w, spreads, hots):
    assemble(flags, part, sf, e, o, f, b, w, spreads, hots, None)


def next_kernel(flags, part, sf, m_next, inv, e, o, f, b, send_columns,
                w, u, pay_e, pay_o, pay_f, pay_b, uown, spreads):
    assemble(flags, part, sf, e, o, f, b, w, spreads, None, send_columns)
    apply_blocks(inv, w, u)
    send_payloads(flags[0], u, m_next[...], sf, pay_e, pay_o, pay_f, pay_b, uown)


def last_kernel(flags, part, sf, e, o, f, b, send_columns, w0, w1, w2, m0, m1, m2, m3,
                sums, w3, spreads):
    assemble(flags, part, sf, e, o, f, b, w3, spreads, None, send_columns)
    fields, mults = [w0, w1, w2, w3], [m0, m1, m2, m3]
    lane = lax.broadcasted_iota(i32, (1, LANES), 1)
    row = jnp.zeros((1, LANES), f32)
    place = 0
    for i in range(4):
        for j in range(i, 4):
            prod = fields[i][...] * fields[j][...]
            prod = jnp.sum(prod, axis=0)
            total = jnp.sum(prod, axis=0, keepdims=True) + jnp.sum(
                mults[i][...] * mults[j][...], axis=0, keepdims=True
            )
            row = jnp.where(lane == place, jnp.sum(total, axis=1, keepdims=True), row)
            place += 1
    sums[...] = row


def finish_kernel(sums, u0, u1, u2, m0, m1, m2, disp, mult, good):
    whole = jnp.sum(jnp.sum(sums[...], axis=0), axis=0, keepdims=True)
    gram = {}
    place = 0
    for i in range(4):
        for j in range(i, 4):
            gram[i, j] = whole[0:1, place : place + 1]
            place += 1
    scale = [lax.rsqrt(gram[i, i]) for i in range(4)]
    scale = [s * (1.5 - 0.5 * ((gram[i, i] * s) * s)) for i, s in enumerate(scale)]
    norm = {(i, j): (gram[i, j] * scale[i]) * scale[j] for i, j in gram}
    d1 = norm[1, 1]
    l21 = norm[1, 2] / d1
    l31 = norm[1, 3] / d1
    d2 = norm[2, 2] - l21 * norm[1, 2]
    t32 = norm[2, 3] - l21 * norm[1, 3]
    l32 = t32 / d2
    d3 = norm[3, 3] - l31 * norm[1, 3] - l32 * t32
    z1 = norm[0, 1]
    z2 = norm[0, 2] - l21 * z1
    z3 = norm[0, 3] - l31 * z1 - l32 * z2
    y3 = z3 / d3
    y2 = z2 / d2 - l32 * y3
    y1 = z1 / d1 - l21 * y2 - l31 * y3
    root = gram[0, 0] * scale[0]
    coef = [y1 * (root * scale[1]), y2 * (root * scale[2]), y3 * (root * scale[3])]
    ok = (d2 > PIVOT_MIN) & (d3 > PIVOT_MIN)
    for i in range(4):
        ok = ok & (gram[i, i] > 1e-25) & (gram[i, i] < 1e37)
    good[...] = jnp.where(ok, 1, 0)
    for c in range(3):
        disp[c] = coef[0] * u0[c] + coef[1] * u1[c] + coef[2] * u2[c]
        rows = slice(4 * c, 4 * c + 4)
        mult[c] = coef[0] * m0[rows, :] + coef[1] * m1[rows, :] + coef[2] * m2[rows, :]


def exchange(pay_e, pay_o, pay_f, pay_b):
    count_x, count_y = lax.axis_size("px"), lax.axis_size("py")
    pairs = [(i, i ^ 1) for i in range(count_x)]
    others = [(i, (((i + 1) ^ 1) - 1) % count_x) for i in range(count_x)]
    forward = [(i, (i + 1) % count_y) for i in range(count_y)]
    backward = [(i, (i - 1) % count_y) for i in range(count_y)]
    return (
        lax.ppermute(pay_e, "px", pairs),
        lax.ppermute(pay_o, "px", others),
        lax.ppermute(pay_f, "py", forward),
        lax.ppermute(pay_b, "py", backward),
    )


def half_operator(flags, u, m, uown, pays, nodes, moduli, stiff, sf, columns=None):
    came = exchange(*pays)
    (got,) = call(local_kernel, [shape(3, 112, LANES)], [u, nodes], flops=20_000_000)
    hots = [pltpu.VMEM((256, 116 * LANES), bf16)] if columns is None else []
    part, m_next, *pays = call(
        element_kernel if columns is None else late_element_kernel,
        [shape(48, 256), shape(12, LANES)] + [shape(8, LANES)] * 4,
        [flags, got, nodes, moduli, stiff, sf, m, uown, *came] + ([] if columns is None else [columns]),
        scratch=[
            pltpu.VMEM((3, 8, LANES), f32),
            pltpu.VMEM((3, 112, LANES), f32),
            pltpu.VMEM((96, 512), f32),
            pltpu.VMEM((96, 512), f32),
            pltpu.VMEM((128, 116 * LANES), bf16),
            *hots,
            pltpu.VMEM((16, 256), f32),
        ],
        smem_first=True,
    )
    return part, exchange(*pays), m_next


SMALL = [pltpu.VMEM((96, 8 * LANES), bf16), pltpu.VMEM((256, 8 * LANES), bf16)]
PAYLOADS = [shape(32, LANES), shape(8, LANES), shape(8, LANES), shape(8, LANES), shape(12, LANES)]


def least_squares(columns, beta):
    cosines, sines, upper = ([], [], [])
    target = [beta] + [jnp.zeros_like(beta) for later in columns]
    for position, column in enumerate(columns):
        column = list(column)
        for earlier in range(position):
            top = cosines[earlier] * column[earlier] + sines[earlier] * column[earlier + 1]
            below = -sines[earlier] * column[earlier] + cosines[earlier] * column[earlier + 1]
            column[earlier] = top
            column[earlier + 1] = below
        pivot = column[position]
        under = column[position + 1]
        radius = jnp.sqrt(pivot * pivot + under * under)
        cosine = pivot / radius
        sine = under / radius
        column[position] = radius
        cosines.append(cosine)
        sines.append(sine)
        target[position + 1] = -sine * target[position]
        target[position] = cosine * target[position]
        upper.append(column)
    count = len(columns)
    coeffs = [None] * count
    for row_index in reversed(range(count)):
        total = target[row_index]
        for later in range(row_index + 1, count):
            total = total - upper[later][row_index] * coeffs[later]
        coeffs[row_index] = total / upper[row_index][row_index]
    return coeffs


def inner(first, second):
    total = jnp.sum(first[0] * second[0]) + jnp.sum(first[1] * second[1])
    return lax.psum(total, ("px", "py"))


def apply_kernel(flags, w, m, inv, sf, u, pay_e, pay_o, pay_f, pay_b, uown):
    apply_blocks(inv, w, u)
    send_payloads(flags[0], u, m[...], sf, pay_e, pay_o, pay_f, pay_b, uown)


def step_by_step(flags, w0, m0, inv, nodes, moduli, stiff, sf):
    def operate(w, m):
        u, *pays, uown = call(
            apply_kernel, [shape(3, ROWS, LANES)] + PAYLOADS, [flags, w, m, inv, sf], smem_first=True
        )
        part, back, m_next = half_operator(flags, u, m, uown, pays, nodes, moduli, stiff, sf)
        (w,) = call(
            alone_kernel, [shape(3, ROWS, LANES)], [flags, part, sf, *back],
            scratch=SMALL, smem_first=True,
        )
        return w, m_next, u

    def step(j, state):
        basis_w, basis_m, solves, entries = state
        last = jnp.maximum(j - 1, 0)
        w, m, u = operate(basis_w[last], basis_m[last])
        w, m = jnp.where(j == 0, w0, w), jnp.where(j == 0, m0, m)

        def remove(i, inside):
            w, m, column = inside
            itself = i == j
            other_w = jnp.where(itself, w, basis_w[i])
            other_m = jnp.where(itself, m, basis_m[i])
            entry = inner((w, m), (other_w, other_m))
            norm = jnp.sqrt(entry)
            w = jnp.where(itself, w / norm, w - entry * other_w)
            m = jnp.where(itself, m / norm, m - entry * other_m)
            return w, m, column.at[i].set(jnp.where(itself, norm, entry))

        w, m, column = lax.fori_loop(0, j + 1, remove, (w, m, jnp.zeros((ITERS + 1,), f32)))
        return (
            basis_w.at[j].set(w), basis_m.at[j].set(m),
            solves.at[last].set(u), entries.at[j].set(column),
        )

    start = (
        jnp.zeros((ITERS + 1,) + w0.shape, f32), jnp.zeros((ITERS + 1,) + m0.shape, f32),
        jnp.zeros((ITERS,) + w0.shape, f32), jnp.zeros((ITERS + 1, ITERS + 1), f32),
    )
    basis_w, basis_m, solves, entries = lax.fori_loop(0, ITERS + 1, step, start)
    columns = [[entries[j, i] for i in range(j + 1)] for j in range(1, ITERS + 1)]
    coeffs = least_squares(columns, entries[0, 0])
    disp = sum(coeffs[j] * solves[j] for j in range(ITERS))
    mult = sum(coeffs[j] * basis_m[j] for j in range(ITERS))
    return disp, mult.reshape(3, 4, LANES)


def body(body_force, fault_slip, elem_nodes, moduli, stiff_ref, block_inv, send_nodes, fault_nodes):
    at_x, at_y = lax.axis_index("px"), lax.axis_index("py")
    count_x, count_y = lax.axis_size("px"), lax.axis_size("py")
    flags = jnp.stack(
        [at_x % 2, at_x > 0, at_x < count_x - 1, at_y > 0, at_y < count_y - 1]
    ).astype(i32)
    w0 = body_force.reshape(3, ROWS, LANES)
    inv = block_inv.reshape(9, ROWS, LANES)
    m0, u, sf, *pays, uown = call(
        first_kernel,
        [shape(12, LANES), shape(3, ROWS, LANES), jax.ShapeDtypeStruct((16, LANES), i32)] + PAYLOADS,
        [flags, w0, fault_slip.reshape(3, 4, LANES), inv, send_nodes[0, 0], fault_nodes[0, 0]],
        smem_first=True,
        grant=LARGE,
    )
    nodes, stiff, lame = call(
        prepare_kernel,
        [jax.ShapeDtypeStruct((112, LANES), i32), jax.ShapeDtypeStruct((192, 288), bf16), shape(2, 512)],
        [elem_nodes.reshape(27, 4, LANES), stiff_ref.transpose(1, 0, 2), moduli[0, 0]],
        grant=LARGE,
    )
    columns = None
    fields, mults, solves = [w0], [m0], []
    for j in range(ITERS):
        solves.append(u)
        part, back, m = half_operator(
            flags, u, mults[-1], uown, pays, nodes, lame, stiff, sf, columns
        )
        mults.append(m)
        if columns is None:
            columns, send_columns = call(
                columns_kernel,
                [
                    jax.ShapeDtypeStruct((116 * LANES, 256), bf16),
                    jax.ShapeDtypeStruct((8 * LANES, 256), bf16),
                ],
                [nodes, sf, part], flops=20_000_000,
            )
        if j < ITERS - 1:
            w, u, *pays, uown = call(
                next_kernel, [shape(3, ROWS, LANES)] * 2 + PAYLOADS,
                [flags, part, sf, m, inv, *back, send_columns], scratch=SMALL[:1], smem_first=True,
            )
            fields.append(w)
    count = count_x * count_y
    (sums,) = call(
        last_kernel, [shape(1, LANES)], [flags, part, sf, *back, send_columns, *fields, *mults],
        scratch=[pltpu.VMEM((3, ROWS, LANES), f32)] + SMALL[:1], smem_first=True,
    )
    sums = lax.all_to_all(
        jnp.broadcast_to(sums[None], (count, 1, LANES)), ("px", "py"), 0, 0
    )
    disp, mult, good = call(
        finish_kernel,
        [shape(3, ROWS, LANES), shape(3, 4, LANES), jax.ShapeDtypeStruct((1, 1), i32)],
        [sums.reshape(count // 8, 8, LANES), *solves, *mults[:ITERS]],
    )
    disp, mult, good = lax.while_loop(
        lambda state: state[2][0, 0] == 0,
        lambda state: (
            *step_by_step(flags, w0, m0, inv, nodes, lame, stiff, sf), jnp.ones((1, 1), i32)
        ),
        (disp, mult, good),
    )
    return (disp.reshape(body_force.shape), mult.reshape(fault_slip.shape))


def solution(mesh):
    split = P("px", "py", None, None)
    in_specs = (split, split, split, split, P(), split, split, split)
    return jax.shard_map(
        body, mesh=mesh, in_specs=in_specs, out_specs=(split, split), check_vma=False
    )
```

```python
import jax
import jax.numpy as jnp
from jax import lax
from jax.experimental import pallas as pl
from jax.experimental.pallas import tpu as pltpu
from jax.sharding import PartitionSpec as P

ITERS = 3
LANES = 128
ROWS = 32
PIVOT_MIN = 0.01
LARGE = 54
f32, bf16, i32, i16 = jnp.float32, jnp.bfloat16, jnp.int32, jnp.int16
highest = lax.Precision.HIGHEST

VMEM = pl.BlockSpec(memory_space=pltpu.VMEM)
SMEM = pl.BlockSpec(memory_space=pltpu.SMEM)


def shape(*dims):
    return jax.ShapeDtypeStruct(dims, f32)


def call(kernel, outs, args, scratch=(), smem_first=False, flops=2_000_000, grant=24):
    specs = [VMEM] * len(args)
    if smem_first:
        specs[0] = SMEM
    return pl.pallas_call(
        kernel,
        out_shape=outs,
        in_specs=specs,
        out_specs=[VMEM] * len(outs),
        scratch_shapes=list(scratch),
        compiler_params=pltpu.CompilerParams(vmem_limit_bytes=grant * 1024 * 1024),
        cost_estimate=pl.CostEstimate(flops=flops, bytes_accessed=1_000_000, transcendentals=0),
    )(*args)


def take_lanes(row, lanes):
    return jnp.take_along_axis(
        jnp.broadcast_to(row, lanes.shape), lanes, axis=1, mode="promise_in_bounds"
    )


def gather_rows(table, first, count, high, low, start):
    acc = [list(per) for per in start]
    for r in range(count):
        rows = [table(c, r) for c in range(3)]
        for n in range(len(high)):
            here = high[n] == r + first
            for c in range(3):
                acc[n][c] = jnp.where(here, take_lanes(rows[c], low[n]), acc[n][c])
    return acc


def pair_rows(row):
    return jnp.broadcast_to(row, (16, row.shape[1]))


def one_hot_low(low_row):
    width = low_row.shape[1]
    low = pair_rows(low_row).astype(i16)
    rows = lax.broadcasted_iota(i16, (16, width), 0)
    one, zero = jnp.ones((16, width), bf16), jnp.zeros((16, width), bf16)
    return [jnp.where(rows + i16(16 * g) == low, one, zero) for g in range(16)]


def spread(high_row, values, with_ghost):
    width = high_row.shape[1]
    high = pair_rows(high_row).astype(i16)
    rows = lax.broadcasted_iota(i16, (16, width), 0)
    here = rows == high
    zero = jnp.zeros((16, width), bf16)
    wide = [pair_rows(value) for value in values]
    tops = [value.astype(bf16) for value in wide]
    lows = [(value - top.astype(f32)).astype(bf16) for value, top in zip(wide, tops)]
    parts = [jnp.where(here, value, zero) for value in tops + lows]
    if with_ghost:
        ghost = jnp.where(rows < 12, (rows & 3) + i16(16), i16(-1)) == high
        for v in (tops, lows):
            whole = jnp.where(rows < 4, v[0], jnp.where(rows < 8, v[1], v[2]))
            parts.append(jnp.where(ghost, whole, zero))
    return parts


def place_chunk(spreads, hots, chunk, index_row, values, with_ghost):
    lanes = slice(LANES * chunk, LANES * chunk + LANES)
    for g, part in enumerate(spread(index_row >> 8, values, with_ghost)):
        spreads[16 * g : 16 * g + 16, lanes] = part
    if hots is None:
        return
    for g, part in enumerate(one_hot_low(index_row & 255)):
        hots[16 * g : 16 * g + 16, lanes] = part


def scatter_product(spreads, hots):
    return lax.dot_general(
        hots[...], spreads[...], (((1,), (1,)), ((), ())), preferred_element_type=f32
    ).T


def send_payloads(par, par_y, u_ref, m_rows, sf, pay_e, pay_o, pay_f, pay_b, uown):
    index = [sf[0:8, :], sf[8:16, :]]
    high = [x >> 7 for x in index]
    low = [x & 127 for x in index]
    zero = jnp.zeros((8, LANES), f32)
    got = gather_rows(
        lambda c, r: u_ref[c, r : r + 1, :], 0, ROWS, high, low, [[zero] * 3, [zero] * 3]
    )
    pad = jnp.zeros((2, LANES), f32)
    sides = [
        jnp.concatenate([got[0][c][2 * s : 2 * s + 2, :] for c in range(3)] + [pad], axis=0)
        for s in range(4)
    ]
    odd = par == 1
    pay_e[0:8, :] = jnp.where(odd, sides[0], sides[1])
    pay_o[...] = jnp.where(odd, sides[1], sides[0])
    odd_y = par_y == 1
    pay_f[...] = jnp.where(odd_y, sides[2], sides[3])
    pay_b[...] = jnp.where(odd_y, sides[3], sides[2])
    for c in range(3):
        uown[4 * c : 4 * c + 4, :] = got[1][c][0:4, :]
        pay_e[8 + 4 * c : 12 + 4 * c, :] = got[1][c][4:8, :]
    pay_e[20:32, :] = m_rows


def apply_blocks(inv_ref, w_ref, u_ref):
    w = [w_ref[c] for c in range(3)]
    for i in range(3):
        u_ref[i] = inv_ref[3 * i] * w[0] + inv_ref[3 * i + 1] * w[1] + inv_ref[3 * i + 2] * w[2]


def from_sides(flags, e, o, f, b):
    odd = flags[0] == 1
    zero = jnp.zeros((8, LANES), f32)
    odd_y = flags[5] == 1
    e, o, f, b = e[0:8, :], o[...], f[...], b[...]
    return [
        jnp.where(flags[1] == 1, jnp.where(odd, e, o), zero),
        jnp.where(flags[2] == 1, jnp.where(odd, o, e), zero),
        jnp.where(flags[3] == 1, jnp.where(odd_y, f, b), zero),
        jnp.where(flags[4] == 1, jnp.where(odd_y, b, f), zero),
    ]


def first_kernel(flags, w, slip, inv, send, fault, m, u, sf, pay_e, pay_o, pay_f, pay_b, uown):
    for c in range(3):
        m[4 * c : 4 * c + 4, :] = slip[c]
    for s in range(4):
        for h in range(2):
            sf[2 * s + h : 2 * s + h + 1, :] = send[s : s + 1, LANES * h : LANES * h + LANES]
    for k in range(2):
        for t in range(4):
            row = 8 + 4 * k + t
            sf[row : row + 1, :] = fault[k : k + 1, LANES * t : LANES * t + LANES]
    apply_blocks(inv, w, u)
    send_payloads(flags[0], flags[5], u, m[...], sf, pay_e, pay_o, pay_f, pay_b, uown)


def prepare_kernel(nodes, stiff, moduli, nodes_out, stiff_out, moduli_out):
    moduli_out[...] = moduli[...]
    for a in range(27):
        nodes_out[4 * a : 4 * a + 4, :] = nodes[a]
    nodes_out[108:112, :] = jnp.zeros((4, LANES), i32)
    rows = lax.broadcasted_iota(i32, (96, 81), 0)
    cols = lax.broadcasted_iota(i32, (96, 81), 1)
    a = rows & 31
    widen = jnp.where(((rows >> 5) * 27 + a == cols) & (a < 27), 1.0, 0.0)
    for k in range(2):
        part = jnp.dot(widen, stiff[:, k, :], precision=highest, preferred_element_type=f32)
        part = lax.dot_general(
            part, widen, (((1,), (1,)), ((), ())), precision=highest, preferred_element_type=f32
        )
        top = part.astype(bf16)
        low = (part - top.astype(f32)).astype(bf16)
        stiff_out[96 * k : 96 * k + 96, :] = jnp.concatenate([top, top, low], axis=1)


def local_kernel(u, nodes, got):
    zero = jnp.zeros((8, LANES), f32)
    for i in range(14):
        index = nodes[8 * i : 8 * i + 8, :]
        (acc,) = gather_rows(
            lambda c, r: u[c, r : r + 1, :], 0, ROWS, [index >> 7], [index & 127], [[zero] * 3]
        )
        for c in range(3):
            got[c, 8 * i : 8 * i + 8, :] = acc[c]


def columns_kernel(nodes, sf, after, hots, send_hots):
    low = jnp.concatenate(
        [nodes[0:108, :], sf[8:16, :], sf[0:8, :], jnp.zeros((4, LANES), i32)], axis=0
    )
    low = (low & 255).astype(f32).T
    lanes = lax.broadcasted_iota(i32, (LANES, 256), 1).astype(f32)
    for chunk in range(124):
        column = jnp.broadcast_to(low[:, chunk : chunk + 1], (LANES, 256))
        made = jnp.where(lanes == column, 1.0, 0.0).astype(bf16)
        dst, place = (hots, chunk) if chunk < 116 else (send_hots, chunk - 116)
        dst[LANES * place : LANES * place + LANES, :] = made


def late_element_kernel(flags, got, nodes, moduli, stiff, sf, m, uown, e, o, f, b, columns,
                        part, m_next, pay_e, pay_o, pay_f, pay_b, ghost, full, wide, r, spreads, out):
    element_kernel(
        flags, got, nodes, moduli, stiff, sf, m, uown, e, o, f, b,
        part, m_next, pay_e, pay_o, pay_f, pay_b, ghost, full, wide, r, spreads, None, out, columns,
    )


def element_kernel(flags, got, nodes, moduli, stiff, sf, m, uown, e, o, f, b,
                   part, m_next, pay_e, pay_o, pay_f, pay_b, ghost, full, wide, r, spreads, hots, out,
                   columns=None):
    sides = from_sides(flags, e, o, f, b)
    for k in range(4):
        for c in range(3):
            ghost[c, 2 * k : 2 * k + 2, :] = sides[k][2 * c : 2 * c + 2, :]
    m_next[...] = uown[...] - e[8:20, :]
    for i in range(14):
        rows = slice(8 * i, 8 * i + 8)
        index = nodes[rows, :]
        (acc,) = gather_rows(
            lambda c, r: ghost[c, r : r + 1, :], ROWS, 8, [index >> 7], [index & 127],
            [[got[c, rows, :] for c in range(3)]],
        )
        for c in range(3):
            full[c, rows, :] = acc[c]
    for c in range(3):
        wide[32 * c + 24 : 32 * c + 32, :] = jnp.zeros((8, 512), f32)
        for t in range(4):
            wide[32 * c : 32 * c + 27, LANES * t : LANES * t + LANES] = full[
                c, pl.ds(t, 27, stride=4), :
            ]
    local = wide[...]
    top = local.astype(bf16)
    low = (local - top.astype(f32)).astype(bf16)
    both = jnp.dot(
        stiff[...], jnp.concatenate([top, low, top], axis=0), preferred_element_type=f32
    )
    r[...] = both[0:96] * moduli[0:1, :] + both[96:192] * moduli[1:2, :]
    for a in range(27):
        for t in range(4):
            lanes = slice(LANES * t, LANES * t + LANES)
            row = 4 * a + t
            values = [r[32 * c + a : 32 * c + a + 1, lanes] for c in range(3)]
            place_chunk(spreads, hots, row, nodes[row : row + 1, :], values, True)
    for t in range(8):
        if t < 4:
            values = [m[4 * c + t : 4 * c + t + 1, :] for c in range(3)]
        else:
            values = [-e[16 + 4 * c + t : 17 + 4 * c + t, :] for c in range(3)]
        place_chunk(spreads, hots, 108 + t, sf[8 + t : 9 + t, :], values, True)
    if columns is None:
        total = scatter_product(spreads, hots)
    else:
        total = jnp.dot(spreads[...], columns[...], preferred_element_type=f32)
    part[...] = total[0:48] + total[48:96]
    out[...] = total[96:112] + total[112:128]
    odd = flags[0] == 1
    odd_y = flags[5] == 1
    for dst in (pay_e, pay_o, pay_f, pay_b):
        dst[6:8, :] = jnp.zeros((2, LANES), f32)
    for c in range(3):
        for h in range(2):
            lane = slice(LANES * h, LANES * h + LANES)
            blocks = [out[4 * c + k : 4 * c + k + 1, lane] for k in range(4)]
            row = slice(2 * c + h, 2 * c + h + 1)
            pay_e[row, :] = jnp.where(odd, blocks[0], blocks[1])
            pay_o[row, :] = jnp.where(odd, blocks[1], blocks[0])
            pay_f[row, :] = jnp.where(odd_y, blocks[2], blocks[3])
            pay_b[row, :] = jnp.where(odd_y, blocks[3], blocks[2])


def assemble(flags, part, sf, e, o, f, b, w, spreads, hots, send_columns):
    sides = from_sides(flags, e, o, f, b)
    for s in range(4):
        for h in range(2):
            row = 2 * s + h
            values = [sides[s][2 * c + h : 2 * c + h + 1, :] for c in range(3)]
            place_chunk(spreads, hots, row, sf[row : row + 1, :], values, False)
    if send_columns is None:
        total = scatter_product(spreads, hots)
    else:
        total = jnp.dot(spreads[...], send_columns[...], preferred_element_type=f32)
    total = part[...] + total[0:48] + total[48:96]
    for c in range(3):
        for h in range(2):
            w[c, pl.ds(h, 16, stride=2), :] = total[
                16 * c : 16 * c + 16, LANES * h : LANES * h + LANES
            ]


def alone_kernel(flags, part, sf, e, o, f, b, w, spreads, hots):
    assemble(flags, part, sf, e, o, f, b, w, spreads, hots, None)


def next_kernel(flags, part, sf, m_next, inv, e, o, f, b, send_columns,
                w, u, pay_e, pay_o, pay_f, pay_b, uown, spreads):
    assemble(flags, part, sf, e, o, f, b, w, spreads, None, send_columns)
    apply_blocks(inv, w, u)
    send_payloads(flags[0], flags[5], u, m_next[...], sf, pay_e, pay_o, pay_f, pay_b, uown)


def last_kernel(flags, part, sf, e, o, f, b, send_columns, w0, w1, w2, m0, m1, m2, m3,
                sums, w3, spreads):
    assemble(flags, part, sf, e, o, f, b, w3, spreads, None, send_columns)
    fields, mults = [w0, w1, w2, w3], [m0, m1, m2, m3]
    lane = lax.broadcasted_iota(i32, (1, LANES), 1)
    row = jnp.zeros((1, LANES), f32)
    place = 0
    for i in range(4):
        for j in range(i, 4):
            prod = fields[i][...] * fields[j][...]
            prod = jnp.sum(prod, axis=0)
            total = jnp.sum(prod, axis=0, keepdims=True) + jnp.sum(
                mults[i][...] * mults[j][...], axis=0, keepdims=True
            )
            row = jnp.where(lane == place, jnp.sum(total, axis=1, keepdims=True), row)
            place += 1
    sums[...] = row


def finish_kernel(sums, u0, u1, u2, m0, m1, m2, disp, mult, good):
    whole = jnp.sum(jnp.sum(sums[...], axis=0), axis=0, keepdims=True)
    gram = {}
    place = 0
    for i in range(4):
        for j in range(i, 4):
            gram[i, j] = whole[0:1, place : place + 1]
            place += 1
    scale = [lax.rsqrt(gram[i, i]) for i in range(4)]
    scale = [s * (1.5 - 0.5 * ((gram[i, i] * s) * s)) for i, s in enumerate(scale)]
    norm = {(i, j): (gram[i, j] * scale[i]) * scale[j] for i, j in gram}
    d1 = norm[1, 1]
    l21 = norm[1, 2] / d1
    l31 = norm[1, 3] / d1
    d2 = norm[2, 2] - l21 * norm[1, 2]
    t32 = norm[2, 3] - l21 * norm[1, 3]
    l32 = t32 / d2
    d3 = norm[3, 3] - l31 * norm[1, 3] - l32 * t32
    z1 = norm[0, 1]
    z2 = norm[0, 2] - l21 * z1
    z3 = norm[0, 3] - l31 * z1 - l32 * z2
    y3 = z3 / d3
    y2 = z2 / d2 - l32 * y3
    y1 = z1 / d1 - l21 * y2 - l31 * y3
    root = gram[0, 0] * scale[0]
    coef = [y1 * (root * scale[1]), y2 * (root * scale[2]), y3 * (root * scale[3])]
    ok = (d2 > PIVOT_MIN) & (d3 > PIVOT_MIN)
    for i in range(4):
        ok = ok & (gram[i, i] > 1e-25) & (gram[i, i] < 1e37)
    good[...] = jnp.where(ok, 1, 0)
    for c in range(3):
        disp[c] = coef[0] * u0[c] + coef[1] * u1[c] + coef[2] * u2[c]
        rows = slice(4 * c, 4 * c + 4)
        mult[c] = coef[0] * m0[rows, :] + coef[1] * m1[rows, :] + coef[2] * m2[rows, :]


def exchange(pay_e, pay_o, pay_f, pay_b):
    count_x, count_y = lax.axis_size("px"), lax.axis_size("py")
    def pairs(count):
        return [(i, i ^ 1) for i in range(count)]

    def others(count):
        return [(i, (((i + 1) ^ 1) - 1) % count) for i in range(count)]

    came_f = lax.ppermute(pay_f, "py", pairs(count_y))
    came_b = lax.ppermute(pay_b, "py", others(count_y))
    came_e = lax.ppermute(pay_e, "px", pairs(count_x))
    came_o = lax.ppermute(pay_o, "px", others(count_x))
    return came_e, came_o, came_f, came_b


def half_operator(flags, u, m, uown, pays, nodes, moduli, stiff, sf, columns=None):
    came = exchange(*pays)
    (got,) = call(local_kernel, [shape(3, 112, LANES)], [u, nodes], flops=20_000_000)
    hots = [pltpu.VMEM((256, 116 * LANES), bf16)] if columns is None else []
    part, m_next, *pays = call(
        element_kernel if columns is None else late_element_kernel,
        [shape(48, 256), shape(12, LANES)] + [shape(8, LANES)] * 4,
        [flags, got, nodes, moduli, stiff, sf, m, uown, *came] + ([] if columns is None else [columns]),
        scratch=[
            pltpu.VMEM((3, 8, LANES), f32),
            pltpu.VMEM((3, 112, LANES), f32),
            pltpu.VMEM((96, 512), f32),
            pltpu.VMEM((96, 512), f32),
            pltpu.VMEM((128, 116 * LANES), bf16),
            *hots,
            pltpu.VMEM((16, 256), f32),
        ],
        smem_first=True,
    )
    return part, exchange(*pays), m_next


SMALL = [pltpu.VMEM((96, 8 * LANES), bf16), pltpu.VMEM((256, 8 * LANES), bf16)]
PAYLOADS = [shape(32, LANES), shape(8, LANES), shape(8, LANES), shape(8, LANES), shape(12, LANES)]


def least_squares(columns, beta):
    cosines, sines, upper = ([], [], [])
    target = [beta] + [jnp.zeros_like(beta) for later in columns]
    for position, column in enumerate(columns):
        column = list(column)
        for earlier in range(position):
            top = cosines[earlier] * column[earlier] + sines[earlier] * column[earlier + 1]
            below = -sines[earlier] * column[earlier] + cosines[earlier] * column[earlier + 1]
            column[earlier] = top
            column[earlier + 1] = below
        pivot = column[position]
        under = column[position + 1]
        radius = jnp.sqrt(pivot * pivot + under * under)
        cosine = pivot / radius
        sine = under / radius
        column[position] = radius
        cosines.append(cosine)
        sines.append(sine)
        target[position + 1] = -sine * target[position]
        target[position] = cosine * target[position]
        upper.append(column)
    count = len(columns)
    coeffs = [None] * count
    for row_index in reversed(range(count)):
        total = target[row_index]
        for later in range(row_index + 1, count):
            total = total - upper[later][row_index] * coeffs[later]
        coeffs[row_index] = total / upper[row_index][row_index]
    return coeffs


def inner(first, second):
    total = jnp.sum(first[0] * second[0]) + jnp.sum(first[1] * second[1])
    return lax.psum(total, ("px", "py"))


def apply_kernel(flags, w, m, inv, sf, u, pay_e, pay_o, pay_f, pay_b, uown):
    apply_blocks(inv, w, u)
    send_payloads(flags[0], flags[5], u, m[...], sf, pay_e, pay_o, pay_f, pay_b, uown)


def step_by_step(flags, w0, m0, inv, nodes, moduli, stiff, sf):
    def operate(w, m):
        u, *pays, uown = call(
            apply_kernel, [shape(3, ROWS, LANES)] + PAYLOADS, [flags, w, m, inv, sf], smem_first=True
        )
        part, back, m_next = half_operator(flags, u, m, uown, pays, nodes, moduli, stiff, sf)
        (w,) = call(
            alone_kernel, [shape(3, ROWS, LANES)], [flags, part, sf, *back],
            scratch=SMALL, smem_first=True,
        )
        return w, m_next, u

    def step(j, state):
        basis_w, basis_m, solves, entries = state
        last = jnp.maximum(j - 1, 0)
        w, m, u = operate(basis_w[last], basis_m[last])
        w, m = jnp.where(j == 0, w0, w), jnp.where(j == 0, m0, m)

        def remove(i, inside):
            w, m, column = inside
            itself = i == j
            other_w = jnp.where(itself, w, basis_w[i])
            other_m = jnp.where(itself, m, basis_m[i])
            entry = inner((w, m), (other_w, other_m))
            norm = jnp.sqrt(entry)
            w = jnp.where(itself, w / norm, w - entry * other_w)
            m = jnp.where(itself, m / norm, m - entry * other_m)
            return w, m, column.at[i].set(jnp.where(itself, norm, entry))

        w, m, column = lax.fori_loop(0, j + 1, remove, (w, m, jnp.zeros((ITERS + 1,), f32)))
        return (
            basis_w.at[j].set(w), basis_m.at[j].set(m),
            solves.at[last].set(u), entries.at[j].set(column),
        )

    start = (
        jnp.zeros((ITERS + 1,) + w0.shape, f32), jnp.zeros((ITERS + 1,) + m0.shape, f32),
        jnp.zeros((ITERS,) + w0.shape, f32), jnp.zeros((ITERS + 1, ITERS + 1), f32),
    )
    basis_w, basis_m, solves, entries = lax.fori_loop(0, ITERS + 1, step, start)
    columns = [[entries[j, i] for i in range(j + 1)] for j in range(1, ITERS + 1)]
    coeffs = least_squares(columns, entries[0, 0])
    disp = sum(coeffs[j] * solves[j] for j in range(ITERS))
    mult = sum(coeffs[j] * basis_m[j] for j in range(ITERS))
    return disp, mult.reshape(3, 4, LANES)


def body(body_force, fault_slip, elem_nodes, moduli, stiff_ref, block_inv, send_nodes, fault_nodes):
    at_x, at_y = lax.axis_index("px"), lax.axis_index("py")
    count_x, count_y = lax.axis_size("px"), lax.axis_size("py")
    flags = jnp.stack(
        [at_x % 2, at_x > 0, at_x < count_x - 1, at_y > 0, at_y < count_y - 1, at_y % 2]
    ).astype(i32)
    w0 = body_force.reshape(3, ROWS, LANES)
    inv = block_inv.reshape(9, ROWS, LANES)
    m0, u, sf, *pays, uown = call(
        first_kernel,
        [shape(12, LANES), shape(3, ROWS, LANES), jax.ShapeDtypeStruct((16, LANES), i32)] + PAYLOADS,
        [flags, w0, fault_slip.reshape(3, 4, LANES), inv, send_nodes[0, 0], fault_nodes[0, 0]],
        smem_first=True,
        grant=LARGE,
    )
    nodes, stiff, lame = call(
        prepare_kernel,
        [jax.ShapeDtypeStruct((112, LANES), i32), jax.ShapeDtypeStruct((192, 288), bf16), shape(2, 512)],
        [elem_nodes.reshape(27, 4, LANES), stiff_ref.transpose(1, 0, 2), moduli[0, 0]],
        grant=LARGE,
    )
    columns = None
    fields, mults, solves = [w0], [m0], []
    for j in range(ITERS):
        solves.append(u)
        part, back, m = half_operator(
            flags, u, mults[-1], uown, pays, nodes, lame, stiff, sf, columns
        )
        mults.append(m)
        if columns is None:
            columns, send_columns = call(
                columns_kernel,
                [
                    jax.ShapeDtypeStruct((116 * LANES, 256), bf16),
                    jax.ShapeDtypeStruct((8 * LANES, 256), bf16),
                ],
                [nodes, sf, part], flops=20_000_000,
            )
        if j < ITERS - 1:
            w, u, *pays, uown = call(
                next_kernel, [shape(3, ROWS, LANES)] * 2 + PAYLOADS,
                [flags, part, sf, m, inv, *back, send_columns], scratch=SMALL[:1], smem_first=True,
            )
            fields.append(w)
    count = count_x * count_y
    (sums,) = call(
        last_kernel, [shape(1, LANES)], [flags, part, sf, *back, send_columns, *fields, *mults],
        scratch=[pltpu.VMEM((3, ROWS, LANES), f32)] + SMALL[:1], smem_first=True,
    )
    sums = lax.all_to_all(
        jnp.broadcast_to(sums[None], (count, 1, LANES)), ("px", "py"), 0, 0
    )
    disp, mult, good = call(
        finish_kernel,
        [shape(3, ROWS, LANES), shape(3, 4, LANES), jax.ShapeDtypeStruct((1, 1), i32)],
        [sums.reshape(count // 8, 8, LANES), *solves, *mults[:ITERS]],
    )
    disp, mult, good = lax.while_loop(
        lambda state: state[2][0, 0] == 0,
        lambda state: (
            *step_by_step(flags, w0, m0, inv, nodes, lame, stiff, sf), jnp.ones((1, 1), i32)
        ),
        (disp, mult, good),
    )
    return (disp.reshape(body_force.shape), mult.reshape(fault_slip.shape))


def solution(mesh):
    split = P("px", "py", None, None)
    in_specs = (split, split, split, split, P(), split, split, split)
    return jax.shard_map(
        body, mesh=mesh, in_specs=in_specs, out_specs=(split, split), check_vma=False
    )
```

```python
import jax
import jax.numpy as jnp
from jax import lax
from jax.experimental import pallas as pl
from jax.experimental.pallas import tpu as pltpu
from jax.sharding import PartitionSpec as P

ITERS = 3
LANES = 128
ROWS = 32
PIVOT_MIN = 0.01
LARGE = 54
f32, bf16, i32, i16 = jnp.float32, jnp.bfloat16, jnp.int32, jnp.int16
highest = lax.Precision.HIGHEST

VMEM = pl.BlockSpec(memory_space=pltpu.VMEM)
SMEM = pl.BlockSpec(memory_space=pltpu.SMEM)


def shape(*dims):
    return jax.ShapeDtypeStruct(dims, f32)


def call(kernel, outs, args, scratch=(), smem_first=False, flops=2_000_000, grant=24):
    specs = [VMEM] * len(args)
    if smem_first:
        specs[0] = SMEM
    return pl.pallas_call(
        kernel,
        out_shape=outs,
        in_specs=specs,
        out_specs=[VMEM] * len(outs),
        scratch_shapes=list(scratch),
        compiler_params=pltpu.CompilerParams(vmem_limit_bytes=grant * 1024 * 1024),
        cost_estimate=pl.CostEstimate(flops=flops, bytes_accessed=1_000_000, transcendentals=0),
    )(*args)


def take_lanes(row, lanes):
    return jnp.take_along_axis(
        jnp.broadcast_to(row, lanes.shape), lanes, axis=1, mode="promise_in_bounds"
    )


def gather_rows(table, first, count, high, low, start):
    acc = [list(per) for per in start]
    for r in range(count):
        rows = [table(c, r) for c in range(3)]
        for n in range(len(high)):
            here = high[n] == r + first
            for c in range(3):
                acc[n][c] = jnp.where(here, take_lanes(rows[c], low[n]), acc[n][c])
    return acc


def pair_rows(row):
    return jnp.broadcast_to(row, (16, row.shape[1]))


def one_hot_low(low_row):
    width = low_row.shape[1]
    low = pair_rows(low_row).astype(i16)
    rows = lax.broadcasted_iota(i16, (16, width), 0)
    one, zero = jnp.ones((16, width), bf16), jnp.zeros((16, width), bf16)
    return [jnp.where(rows + i16(16 * g) == low, one, zero) for g in range(16)]


def spread(high_row, values, with_ghost):
    width = high_row.shape[1]
    high = pair_rows(high_row).astype(i16)
    rows = lax.broadcasted_iota(i16, (16, width), 0)
    here = rows == high
    zero = jnp.zeros((16, width), bf16)
    wide = [pair_rows(value) for value in values]
    tops = [value.astype(bf16) for value in wide]
    lows = [(value - top.astype(f32)).astype(bf16) for value, top in zip(wide, tops)]
    parts = [jnp.where(here, value, zero) for value in tops + lows]
    if with_ghost:
        ghost = jnp.where(rows < 12, (rows & 3) + i16(16), i16(-1)) == high
        for v in (tops, lows):
            whole = jnp.where(rows < 4, v[0], jnp.where(rows < 8, v[1], v[2]))
            parts.append(jnp.where(ghost, whole, zero))
    return parts


def place_chunk(spreads, hots, chunk, index_row, values, with_ghost):
    lanes = slice(LANES * chunk, LANES * chunk + LANES)
    for g, part in enumerate(spread(index_row >> 8, values, with_ghost)):
        spreads[16 * g : 16 * g + 16, lanes] = part
    if hots is None:
        return
    for g, part in enumerate(one_hot_low(index_row & 255)):
        hots[16 * g : 16 * g + 16, lanes] = part


def scatter_product(spreads, hots):
    return lax.dot_general(
        hots[...], spreads[...], (((1,), (1,)), ((), ())), preferred_element_type=f32
    ).T


def send_payloads(par, par_y, u_ref, m_rows, sf, pay_e, pay_o, pay_f, pay_b, uown):
    index = [sf[0:8, :], sf[8:16, :]]
    high = [x >> 7 for x in index]
    low = [x & 127 for x in index]
    zero = jnp.zeros((8, LANES), f32)
    got = gather_rows(
        lambda c, r: u_ref[c, r : r + 1, :], 0, ROWS, high, low, [[zero] * 3, [zero] * 3]
    )
    pad = jnp.zeros((2, LANES), f32)
    sides = [
        jnp.concatenate([got[0][c][2 * s : 2 * s + 2, :] for c in range(3)] + [pad], axis=0)
        for s in range(4)
    ]
    odd = par == 1
    pay_e[0:8, :] = jnp.where(odd, sides[0], sides[1])
    pay_o[...] = jnp.where(odd, sides[1], sides[0])
    odd_y = par_y == 1
    pay_f[...] = jnp.where(odd_y, sides[2], sides[3])
    pay_b[...] = jnp.where(odd_y, sides[3], sides[2])
    for c in range(3):
        uown[4 * c : 4 * c + 4, :] = got[1][c][0:4, :]
        pay_e[8 + 4 * c : 12 + 4 * c, :] = got[1][c][4:8, :]
    pay_e[20:32, :] = m_rows


def apply_blocks(inv_ref, w_ref, u_ref):
    w = [w_ref[c] for c in range(3)]
    for i in range(3):
        u_ref[i] = inv_ref[3 * i] * w[0] + inv_ref[3 * i + 1] * w[1] + inv_ref[3 * i + 2] * w[2]


def from_sides(flags, e, o, f, b):
    odd = flags[0] == 1
    zero = jnp.zeros((8, LANES), f32)
    odd_y = flags[5] == 1
    e, o, f, b = e[0:8, :], o[...], f[...], b[...]
    return [
        jnp.where(flags[1] == 1, jnp.where(odd, e, o), zero),
        jnp.where(flags[2] == 1, jnp.where(odd, o, e), zero),
        jnp.where(flags[3] == 1, jnp.where(odd_y, f, b), zero),
        jnp.where(flags[4] == 1, jnp.where(odd_y, b, f), zero),
    ]


def first_kernel(flags, w, slip, inv, send, fault, m, u, sf, pay_e, pay_o, pay_f, pay_b, uown):
    for c in range(3):
        m[4 * c : 4 * c + 4, :] = slip[c]
    for s in range(4):
        for h in range(2):
            sf[2 * s + h : 2 * s + h + 1, :] = send[s : s + 1, LANES * h : LANES * h + LANES]
    for k in range(2):
        for t in range(4):
            row = 8 + 4 * k + t
            sf[row : row + 1, :] = fault[k : k + 1, LANES * t : LANES * t + LANES]
    apply_blocks(inv, w, u)
    send_payloads(flags[0], flags[5], u, m[...], sf, pay_e, pay_o, pay_f, pay_b, uown)


def prepare_kernel(nodes, stiff, moduli, nodes_out, stiff_out, moduli_out):
    moduli_out[...] = moduli[...]
    for a in range(27):
        nodes_out[4 * a : 4 * a + 4, :] = nodes[a]
    nodes_out[108:112, :] = jnp.zeros((4, LANES), i32)
    rows = lax.broadcasted_iota(i32, (96, 81), 0)
    cols = lax.broadcasted_iota(i32, (96, 81), 1)
    a = rows & 31
    widen = jnp.where(((rows >> 5) * 27 + a == cols) & (a < 27), 1.0, 0.0)
    for k in range(2):
        part = jnp.dot(widen, stiff[:, k, :], precision=highest, preferred_element_type=f32)
        part = lax.dot_general(
            part, widen, (((1,), (1,)), ((), ())), precision=highest, preferred_element_type=f32
        )
        top = part.astype(bf16)
        low = (part - top.astype(f32)).astype(bf16)
        stiff_out[96 * k : 96 * k + 96, :] = jnp.concatenate([top, top, low], axis=1)


def local_kernel(u, nodes, got):
    zero = jnp.zeros((8, LANES), f32)

    def pair(i, carry):
        for n in range(2):
            rows = pl.ds(pl.multiple_of(16 * i + 8 * n, 8), 8)
            index = nodes[rows, :]
            (acc,) = gather_rows(
                lambda c, r: u[c, r : r + 1, :], 0, ROWS, [index >> 7], [index & 127], [[zero] * 3]
            )
            for c in range(3):
                got[c, rows, :] = acc[c]
        return carry

    lax.fori_loop(0, 7, pair, 0)


def columns_kernel(nodes, sf, after, hots, send_hots):
    low = jnp.concatenate(
        [nodes[0:108, :], sf[8:16, :], sf[0:8, :], jnp.zeros((4, LANES), i32)], axis=0
    )
    low = (low & 255).astype(f32).T
    lanes = lax.broadcasted_iota(i32, (LANES, 256), 1).astype(f32)
    for chunk in range(124):
        column = jnp.broadcast_to(low[:, chunk : chunk + 1], (LANES, 256))
        made = jnp.where(lanes == column, 1.0, 0.0).astype(bf16)
        dst, place = (hots, chunk) if chunk < 116 else (send_hots, chunk - 116)
        dst[LANES * place : LANES * place + LANES, :] = made


def late_element_kernel(flags, got, nodes, moduli, stiff, sf, m, uown, e, o, f, b, columns,
                        part, m_next, pay_e, pay_o, pay_f, pay_b, ghost, full, wide, r, spreads, out):
    element_kernel(
        flags, got, nodes, moduli, stiff, sf, m, uown, e, o, f, b,
        part, m_next, pay_e, pay_o, pay_f, pay_b, ghost, full, wide, r, spreads, None, out, columns,
    )


def element_kernel(flags, got, nodes, moduli, stiff, sf, m, uown, e, o, f, b,
                   part, m_next, pay_e, pay_o, pay_f, pay_b, ghost, full, wide, r, spreads, hots, out,
                   columns=None):
    sides = from_sides(flags, e, o, f, b)
    for k in range(4):
        for c in range(3):
            ghost[c, 2 * k : 2 * k + 2, :] = sides[k][2 * c : 2 * c + 2, :]
    m_next[...] = uown[...] - e[8:20, :]
    for i in range(14):
        rows = slice(8 * i, 8 * i + 8)
        index = nodes[rows, :]
        (acc,) = gather_rows(
            lambda c, r: ghost[c, r : r + 1, :], ROWS, 8, [index >> 7], [index & 127],
            [[got[c, rows, :] for c in range(3)]],
        )
        for c in range(3):
            full[c, rows, :] = acc[c]
    for c in range(3):
        wide[32 * c + 24 : 32 * c + 32, :] = jnp.zeros((8, 512), f32)
        for t in range(4):
            wide[32 * c : 32 * c + 27, LANES * t : LANES * t + LANES] = full[
                c, pl.ds(t, 27, stride=4), :
            ]
    local = wide[...]
    top = local.astype(bf16)
    low = (local - top.astype(f32)).astype(bf16)
    both = jnp.dot(
        stiff[...], jnp.concatenate([top, low, top], axis=0), preferred_element_type=f32
    )
    r[...] = both[0:96] * moduli[0:1, :] + both[96:192] * moduli[1:2, :]
    for a in range(27):
        for t in range(4):
            lanes = slice(LANES * t, LANES * t + LANES)
            row = 4 * a + t
            values = [r[32 * c + a : 32 * c + a + 1, lanes] for c in range(3)]
            place_chunk(spreads, hots, row, nodes[row : row + 1, :], values, True)
    for t in range(8):
        if t < 4:
            values = [m[4 * c + t : 4 * c + t + 1, :] for c in range(3)]
        else:
            values = [-e[16 + 4 * c + t : 17 + 4 * c + t, :] for c in range(3)]
        place_chunk(spreads, hots, 108 + t, sf[8 + t : 9 + t, :], values, True)
    if columns is None:
        total = scatter_product(spreads, hots)
    else:
        total = jnp.dot(spreads[...], columns[...], preferred_element_type=f32)
    part[...] = total[0:48] + total[48:96]
    out[...] = total[96:112] + total[112:128]
    odd = flags[0] == 1
    odd_y = flags[5] == 1
    for dst in (pay_e, pay_o, pay_f, pay_b):
        dst[6:8, :] = jnp.zeros((2, LANES), f32)
    for c in range(3):
        for h in range(2):
            lane = slice(LANES * h, LANES * h + LANES)
            blocks = [out[4 * c + k : 4 * c + k + 1, lane] for k in range(4)]
            row = slice(2 * c + h, 2 * c + h + 1)
            pay_e[row, :] = jnp.where(odd, blocks[0], blocks[1])
            pay_o[row, :] = jnp.where(odd, blocks[1], blocks[0])
            pay_f[row, :] = jnp.where(odd_y, blocks[2], blocks[3])
            pay_b[row, :] = jnp.where(odd_y, blocks[3], blocks[2])


def assemble(flags, part, sf, e, o, f, b, w, spreads, hots, send_columns):
    sides = from_sides(flags, e, o, f, b)
    for s in range(4):
        for h in range(2):
            row = 2 * s + h
            values = [sides[s][2 * c + h : 2 * c + h + 1, :] for c in range(3)]
            place_chunk(spreads, hots, row, sf[row : row + 1, :], values, False)
    if send_columns is None:
        total = scatter_product(spreads, hots)
    else:
        total = jnp.dot(spreads[...], send_columns[...], preferred_element_type=f32)
    total = part[...] + total[0:48] + total[48:96]
    for c in range(3):
        for h in range(2):
            w[c, pl.ds(h, 16, stride=2), :] = total[
                16 * c : 16 * c + 16, LANES * h : LANES * h + LANES
            ]


def alone_kernel(flags, part, sf, e, o, f, b, w, spreads, hots):
    assemble(flags, part, sf, e, o, f, b, w, spreads, hots, None)


def next_kernel(flags, part, sf, m_next, inv, e, o, f, b, send_columns,
                w, u, pay_e, pay_o, pay_f, pay_b, uown, spreads):
    assemble(flags, part, sf, e, o, f, b, w, spreads, None, send_columns)
    apply_blocks(inv, w, u)
    send_payloads(flags[0], flags[5], u, m_next[...], sf, pay_e, pay_o, pay_f, pay_b, uown)


def last_kernel(flags, part, sf, e, o, f, b, send_columns, w0, w1, w2, m0, m1, m2, m3,
                sums, w3, spreads):
    assemble(flags, part, sf, e, o, f, b, w3, spreads, None, send_columns)
    fields, mults = [w0, w1, w2, w3], [m0, m1, m2, m3]
    lane = lax.broadcasted_iota(i32, (1, LANES), 1)
    row = jnp.zeros((1, LANES), f32)
    place = 0
    for i in range(4):
        for j in range(i, 4):
            prod = fields[i][...] * fields[j][...]
            prod = jnp.sum(prod, axis=0)
            total = jnp.sum(prod, axis=0, keepdims=True) + jnp.sum(
                mults[i][...] * mults[j][...], axis=0, keepdims=True
            )
            row = jnp.where(lane == place, jnp.sum(total, axis=1, keepdims=True), row)
            place += 1
    sums[...] = row


def finish_kernel(sums, u0, u1, u2, m0, m1, m2, disp, mult, good):
    whole = jnp.sum(jnp.sum(sums[...], axis=0), axis=0, keepdims=True)
    gram = {}
    place = 0
    for i in range(4):
        for j in range(i, 4):
            gram[i, j] = whole[0:1, place : place + 1]
            place += 1
    scale = [lax.rsqrt(gram[i, i]) for i in range(4)]
    scale = [s * (1.5 - 0.5 * ((gram[i, i] * s) * s)) for i, s in enumerate(scale)]
    norm = {(i, j): (gram[i, j] * scale[i]) * scale[j] for i, j in gram}
    d1 = norm[1, 1]
    l21 = norm[1, 2] / d1
    l31 = norm[1, 3] / d1
    d2 = norm[2, 2] - l21 * norm[1, 2]
    t32 = norm[2, 3] - l21 * norm[1, 3]
    l32 = t32 / d2
    d3 = norm[3, 3] - l31 * norm[1, 3] - l32 * t32
    z1 = norm[0, 1]
    z2 = norm[0, 2] - l21 * z1
    z3 = norm[0, 3] - l31 * z1 - l32 * z2
    y3 = z3 / d3
    y2 = z2 / d2 - l32 * y3
    y1 = z1 / d1 - l21 * y2 - l31 * y3
    root = gram[0, 0] * scale[0]
    coef = [y1 * (root * scale[1]), y2 * (root * scale[2]), y3 * (root * scale[3])]
    ok = (d2 > PIVOT_MIN) & (d3 > PIVOT_MIN)
    for i in range(4):
        ok = ok & (gram[i, i] > 1e-25) & (gram[i, i] < 1e37)
    good[...] = jnp.where(ok, 1, 0)
    for c in range(3):
        disp[c] = coef[0] * u0[c] + coef[1] * u1[c] + coef[2] * u2[c]
        rows = slice(4 * c, 4 * c + 4)
        mult[c] = coef[0] * m0[rows, :] + coef[1] * m1[rows, :] + coef[2] * m2[rows, :]


def exchange(pay_e, pay_o, pay_f, pay_b):
    count_x, count_y = lax.axis_size("px"), lax.axis_size("py")
    def pairs(count):
        return [(i, i ^ 1) for i in range(count)]

    def others(count):
        return [(i, (((i + 1) ^ 1) - 1) % count) for i in range(count)]

    came_f = lax.ppermute(pay_f, "py", pairs(count_y))
    came_b = lax.ppermute(pay_b, "py", others(count_y))
    came_e = lax.ppermute(pay_e, "px", pairs(count_x))
    came_o = lax.ppermute(pay_o, "px", others(count_x))
    return came_e, came_o, came_f, came_b


def exchange_rotating(pay_e, pay_o, pay_f, pay_b):
    count_x, count_y = lax.axis_size("px"), lax.axis_size("py")
    pairs = [(i, i ^ 1) for i in range(count_x)]
    others = [(i, (((i + 1) ^ 1) - 1) % count_x) for i in range(count_x)]
    forward = [(i, (i + 1) % count_y) for i in range(count_y)]
    backward = [(i, (i - 1) % count_y) for i in range(count_y)]
    odd = lax.axis_index("py") % 2 == 1
    lower = lax.ppermute(jnp.where(odd, pay_b, pay_f), "py", forward)
    upper = lax.ppermute(jnp.where(odd, pay_f, pay_b), "py", backward)
    return (
        lax.ppermute(pay_e, "px", pairs), lax.ppermute(pay_o, "px", others),
        jnp.where(odd, lower, upper), jnp.where(odd, upper, lower),
    )


def half_operator(flags, u, m, uown, pays, nodes, moduli, stiff, sf, columns=None, swap=exchange):
    came = swap(*pays)
    (got,) = call(local_kernel, [shape(3, 112, LANES)], [u, nodes], flops=20_000_000)
    hots = [pltpu.VMEM((256, 116 * LANES), bf16)] if columns is None else []
    part, m_next, *pays = call(
        element_kernel if columns is None else late_element_kernel,
        [shape(48, 256), shape(12, LANES)] + [shape(8, LANES)] * 4,
        [flags, got, nodes, moduli, stiff, sf, m, uown, *came] + ([] if columns is None else [columns]),
        scratch=[
            pltpu.VMEM((3, 8, LANES), f32),
            pltpu.VMEM((3, 112, LANES), f32),
            pltpu.VMEM((96, 512), f32),
            pltpu.VMEM((96, 512), f32),
            pltpu.VMEM((128, 116 * LANES), bf16),
            *hots,
            pltpu.VMEM((16, 256), f32),
        ],
        smem_first=True,
    )
    return part, swap(*pays), m_next


SMALL = [pltpu.VMEM((96, 8 * LANES), bf16), pltpu.VMEM((256, 8 * LANES), bf16)]
PAYLOADS = [shape(32, LANES), shape(8, LANES), shape(8, LANES), shape(8, LANES), shape(12, LANES)]


def least_squares(columns, beta):
    cosines, sines, upper = ([], [], [])
    target = [beta] + [jnp.zeros_like(beta) for later in columns]
    for position, column in enumerate(columns):
        column = list(column)
        for earlier in range(position):
            top = cosines[earlier] * column[earlier] + sines[earlier] * column[earlier + 1]
            below = -sines[earlier] * column[earlier] + cosines[earlier] * column[earlier + 1]
            column[earlier] = top
            column[earlier + 1] = below
        pivot = column[position]
        under = column[position + 1]
        radius = jnp.sqrt(pivot * pivot + under * under)
        cosine = pivot / radius
        sine = under / radius
        column[position] = radius
        cosines.append(cosine)
        sines.append(sine)
        target[position + 1] = -sine * target[position]
        target[position] = cosine * target[position]
        upper.append(column)
    count = len(columns)
    coeffs = [None] * count
    for row_index in reversed(range(count)):
        total = target[row_index]
        for later in range(row_index + 1, count):
            total = total - upper[later][row_index] * coeffs[later]
        coeffs[row_index] = total / upper[row_index][row_index]
    return coeffs


def inner(first, second):
    total = jnp.sum(first[0] * second[0]) + jnp.sum(first[1] * second[1])
    return lax.psum(total, ("px", "py"))


def apply_kernel(flags, w, m, inv, sf, u, pay_e, pay_o, pay_f, pay_b, uown):
    apply_blocks(inv, w, u)
    send_payloads(flags[0], flags[5], u, m[...], sf, pay_e, pay_o, pay_f, pay_b, uown)


def step_by_step(flags, w0, m0, inv, nodes, moduli, stiff, sf):
    def operate(w, m):
        u, *pays, uown = call(
            apply_kernel, [shape(3, ROWS, LANES)] + PAYLOADS, [flags, w, m, inv, sf], smem_first=True
        )
        part, back, m_next = half_operator(
            flags, u, m, uown, pays, nodes, moduli, stiff, sf, swap=exchange_rotating
        )
        (w,) = call(
            alone_kernel, [shape(3, ROWS, LANES)], [flags, part, sf, *back],
            scratch=SMALL, smem_first=True,
        )
        return w, m_next, u

    def step(j, state):
        basis_w, basis_m, solves, entries = state
        last = jnp.maximum(j - 1, 0)
        w, m, u = operate(basis_w[last], basis_m[last])
        w, m = jnp.where(j == 0, w0, w), jnp.where(j == 0, m0, m)

        def remove(i, inside):
            w, m, column = inside
            itself = i == j
            other_w = jnp.where(itself, w, basis_w[i])
            other_m = jnp.where(itself, m, basis_m[i])
            entry = inner((w, m), (other_w, other_m))
            norm = jnp.sqrt(entry)
            w = jnp.where(itself, w / norm, w - entry * other_w)
            m = jnp.where(itself, m / norm, m - entry * other_m)
            return w, m, column.at[i].set(jnp.where(itself, norm, entry))

        w, m, column = lax.fori_loop(0, j + 1, remove, (w, m, jnp.zeros((ITERS + 1,), f32)))
        return (
            basis_w.at[j].set(w), basis_m.at[j].set(m),
            solves.at[last].set(u), entries.at[j].set(column),
        )

    start = (
        jnp.zeros((ITERS + 1,) + w0.shape, f32), jnp.zeros((ITERS + 1,) + m0.shape, f32),
        jnp.zeros((ITERS,) + w0.shape, f32), jnp.zeros((ITERS + 1, ITERS + 1), f32),
    )
    basis_w, basis_m, solves, entries = lax.fori_loop(0, ITERS + 1, step, start)
    columns = [[entries[j, i] for i in range(j + 1)] for j in range(1, ITERS + 1)]
    coeffs = least_squares(columns, entries[0, 0])
    disp = sum(coeffs[j] * solves[j] for j in range(ITERS))
    mult = sum(coeffs[j] * basis_m[j] for j in range(ITERS))
    return disp, mult.reshape(3, 4, LANES)


def body(body_force, fault_slip, elem_nodes, moduli, stiff_ref, block_inv, send_nodes, fault_nodes):
    at_x, at_y = lax.axis_index("px"), lax.axis_index("py")
    count_x, count_y = lax.axis_size("px"), lax.axis_size("py")
    flags = jnp.stack(
        [at_x % 2, at_x > 0, at_x < count_x - 1, at_y > 0, at_y < count_y - 1, at_y % 2]
    ).astype(i32)
    w0 = body_force.reshape(3, ROWS, LANES)
    inv = block_inv.reshape(9, ROWS, LANES)
    m0, u, sf, *pays, uown = call(
        first_kernel,
        [shape(12, LANES), shape(3, ROWS, LANES), jax.ShapeDtypeStruct((16, LANES), i32)] + PAYLOADS,
        [flags, w0, fault_slip.reshape(3, 4, LANES), inv, send_nodes[0, 0], fault_nodes[0, 0]],
        smem_first=True,
        grant=LARGE,
    )
    nodes, stiff, lame = call(
        prepare_kernel,
        [jax.ShapeDtypeStruct((112, LANES), i32), jax.ShapeDtypeStruct((192, 288), bf16), shape(2, 512)],
        [elem_nodes.reshape(27, 4, LANES), stiff_ref.transpose(1, 0, 2), moduli[0, 0]],
        grant=LARGE,
    )
    columns = None
    fields, mults, solves = [w0], [m0], []
    for j in range(ITERS):
        solves.append(u)
        part, back, m = half_operator(
            flags, u, mults[-1], uown, pays, nodes, lame, stiff, sf, columns
        )
        mults.append(m)
        if columns is None:
            columns, send_columns = call(
                columns_kernel,
                [
                    jax.ShapeDtypeStruct((116 * LANES, 256), bf16),
                    jax.ShapeDtypeStruct((8 * LANES, 256), bf16),
                ],
                [nodes, sf, part], flops=20_000_000,
            )
        if j < ITERS - 1:
            w, u, *pays, uown = call(
                next_kernel, [shape(3, ROWS, LANES)] * 2 + PAYLOADS,
                [flags, part, sf, m, inv, *back, send_columns], scratch=SMALL[:1], smem_first=True,
            )
            fields.append(w)
    count = count_x * count_y
    (sums,) = call(
        last_kernel, [shape(1, LANES)], [flags, part, sf, *back, send_columns, *fields, *mults],
        scratch=[pltpu.VMEM((3, ROWS, LANES), f32)] + SMALL[:1], smem_first=True,
    )
    sums = lax.all_to_all(
        jnp.broadcast_to(sums[None], (count, 1, LANES)), ("px", "py"), 0, 0
    )
    disp, mult, good = call(
        finish_kernel,
        [shape(3, ROWS, LANES), shape(3, 4, LANES), jax.ShapeDtypeStruct((1, 1), i32)],
        [sums.reshape(count // 8, 8, LANES), *solves, *mults[:ITERS]],
    )
    disp, mult, good = lax.while_loop(
        lambda state: state[2][0, 0] == 0,
        lambda state: (
            *step_by_step(flags, w0, m0, inv, nodes, lame, stiff, sf), jnp.ones((1, 1), i32)
        ),
        (disp, mult, good),
    )
    return (disp.reshape(body_force.shape), mult.reshape(fault_slip.shape))


def solution(mesh):
    split = P("px", "py", None, None)
    in_specs = (split, split, split, split, P(), split, split, split)
    return jax.shard_map(
        body, mesh=mesh, in_specs=in_specs, out_specs=(split, split), check_vma=False
    )
```
